32 devices in a mesh: freq: 2 (over x), geo: 16 (over z, y, core).
Axes of the slice: x: 2, y: 2, z: 4, core: 2. Of those that a mesh axis runs over, the one named last changes fastest.
Arguments:
- energy: float32 [64, 48, 36, 128], P('geo', 'freq'), may hold values from 0.1 to 1.5
- water_depth: float32 [64, 128], P('geo'), may hold values from 0.5 to 4
- wet_mask: int32 [64, 128], P('geo'), may hold values 0 or 1
- vegetation: int32 [64, 128], P('geo'), may hold values 0 or 1
- canopy: float32 [64, 128], P('geo'), may hold values from 0.004 to 0.04
- quad_offsets: int32 [4], replicated, may hold values from 1 to 3, as said below
- quad_weights: float32 [2], replicated, may hold values from 0.2 to 0.8
Outputs:
- energy_next: float32 [64, 48, 36, 128], P('geo', 'freq')
- orbital: float32 [64, 128], P('geo')
The draws below stay inside these ranges and needn't reach their ends.
Inputs may be any that keep to these rules, and one draw needn't show every extreme that they name: `quad_offsets`: offsets a and the two direction turns lie in 1 .. 3; the lower frequency offset b equals 3 in every draw.
All inputs are finite; a program needn't handle non-finite values. No bound on the sum of `wet_mask` or of `vegetation` on one device may be relied on, other than what follows from the above.
Results may differ from the reference program's by a relative error of at most 0.00002.
Values sent between devices are 32-bit elements; how exact they have to be, the bound alone decides.
A program may use at most 64 MiB of HBM per device.

```python
import math
import jax
import jax.numpy as jnp
from jax import lax

FREQS = 48
DIRS = 36
FH = 4
SUBSTEPS = 8
CY = 4
NX = 128
NY = 64


def draw_quad_offsets(key, part):
    keys = jax.random.split(key, 2)
    up_bins = jax.random.randint(keys[0], (1,), 1, FH)
    down_bins = jnp.full((1,), FH - 1, jnp.int32)
    turns = jax.random.randint(keys[1], (2,), 1, FH)
    return jnp.concatenate([up_bins, down_bins, turns]).astype(jnp.int32)


def touch_ends(values, rng, low, high):
    dims = values.shape
    place = [jax.random.randint(jax.random.fold_in(rng, axis), (), 0, dims[axis]) for axis in range(len(dims))]
    values = values.at[tuple(place)].set(low)
    longest = dims.index(max(dims))
    place[longest] = (place[longest] + 1) % dims[longest]
    return values.at[tuple(place)].set(high)


def shard_levels(own_key, dims, shards, low, high):
    gain, own = 1.0, jax.random.fold_in(own_key, 6)
    for axis_at, shards_of in shards:
        steps = jnp.exp(jax.random.uniform(jax.random.fold_in(own, axis_at), (shards_of,), jnp.float32, low / len(shards), high / len(shards)))
        gain = gain * jnp.repeat(steps, dims[axis_at] // shards_of).reshape([-1 if axis == axis_at else 1 for axis in range(len(dims))])
    return gain


def setup_inputs(seed: int = 0) -> dict:
    arg_keys = jax.random.split(jax.random.key(seed), 8)
    return {
        "energy": jnp.clip(jnp.exp(math.log(1.5) - 2.7080502 * jax.random.uniform(arg_keys[0], (NY, FREQS, DIRS, NX), jnp.float32) ** shard_levels(arg_keys[0], (NY, FREQS, DIRS, NX), ((0, 16), (1, 2)), -0.2, 0.2)), 0.1, 1.5),
        "water_depth": jnp.clip(0.5 + 3.5 * jax.random.uniform(arg_keys[1], (NY, NX), jnp.float32) ** shard_levels(arg_keys[1], (NY, NX), ((0, 16),), -0.2, 0.2), 0.5, 4.0),
        "wet_mask": touch_ends((jax.random.randint(arg_keys[2], (NY, NX), 0, 5) < 4).astype(jnp.int32), jax.random.fold_in(arg_keys[2], 1), 0, 1),
        "vegetation": touch_ends((jax.random.randint(arg_keys[3], (NY, NX), 0, 2) < 1).astype(jnp.int32), jax.random.fold_in(arg_keys[3], 1), 0, 1),
        "canopy": jnp.clip(jnp.exp(math.log(0.04) - 2.30258502 * jax.random.uniform(arg_keys[4], (NY, NX), jnp.float32) ** shard_levels(arg_keys[4], (NY, NX), ((0, 16),), -0.2, 0.2)), 0.004, 0.04),
        "quad_offsets": draw_quad_offsets(jax.random.fold_in(arg_keys[7], 71), 0),
        "quad_weights": jnp.clip(jax.random.uniform(arg_keys[6], (2,), jnp.float32, 0.2, 0.8), 0.2, 0.8),
    }


gravity = 9.81
base_freq = 0.03
freq_ratio = 1.05
cell_size = 20.0
sub_step = 2.0
coupling = 0.01
coef_plus = 0.4096
coef_minus = 3.1605
coef_both = 2.589

def physics(radian_freq, water_depth, dir_count):
    square = (radian_freq * radian_freq)[None, :, None]
    column = water_depth[:, None, :]
    depth_ratio = square * column / gravity
    depth_wave = depth_ratio / jnp.sqrt(jnp.tanh(depth_ratio))
    group_speed = radian_freq[None, :, None] * column / depth_wave * (0.5 + depth_wave / jnp.sinh(2.0 * depth_wave))
    orbit_weight = square / jnp.sinh(depth_wave) ** 2 * (radian_freq * (freq_ratio - 1.0))[None, :, None] * (2.0 * math.pi / dir_count)
    return (group_speed, orbit_weight)

def angles_of(dir_count):
    angles = (jnp.arange(dir_count, dtype=jnp.float32) + 0.5) * (2.0 * math.pi / dir_count)
    return (jnp.cos(angles), jnp.sin(angles))

def shifted(doubled, freq_off, dir_off, count):
    dir_count = doubled.shape[2] // 2
    starts = (jnp.zeros((), jnp.int32), (freq_off + FH).astype(jnp.int32), (dir_off % dir_count).astype(jnp.int32), jnp.zeros((), jnp.int32))
    return lax.dynamic_slice(doubled, starts, (doubled.shape[0], count, dir_count, doubled.shape[3]))

def interaction(extended, masked, quad_offsets, quad_weights):
    count = masked.shape[1]
    doubled = jnp.concatenate([extended, extended], axis=2)
    up_bins, down_bins, up_turn, down_turn = (quad_offsets[0], quad_offsets[1], quad_offsets[2], quad_offsets[3])
    weight_up, weight_down = (quad_weights[0], quad_weights[1])
    upper = weight_up * shifted(doubled, up_bins, up_turn, count) + (1.0 - weight_up) * shifted(doubled, up_bins + 1, up_turn, count)
    lower = weight_down * shifted(doubled, -down_bins, -down_turn, count) + (1.0 - weight_down) * shifted(doubled, -down_bins - 1, -down_turn, count)
    return coupling * (masked * masked * (coef_plus * upper + coef_minus * lower) - coef_both * masked * upper * lower)

def redistribute(extended, transfer, quad_offsets, quad_weights):
    count = transfer.shape[1]
    doubled = jnp.concatenate([extended, extended], axis=2)
    up_bins, down_bins, up_turn, down_turn = (quad_offsets[0], quad_offsets[1], quad_offsets[2], quad_offsets[3])
    weight_up, weight_down = (quad_weights[0], quad_weights[1])
    gained = weight_up * shifted(doubled, -up_bins, -up_turn, count) + (1.0 - weight_up) * shifted(doubled, -up_bins - 1, -up_turn, count)
    gained = gained + weight_down * shifted(doubled, down_bins, down_turn, count) + (1.0 - weight_down) * shifted(doubled, down_bins + 1, down_turn, count)
    return gained - 2.0 * transfer

def east_west(east_flux, cosines):
    zeros = jnp.zeros_like(east_flux[..., :1])
    behind = jnp.concatenate([zeros, east_flux[..., :-1]], axis=-1)
    ahead = jnp.concatenate([east_flux[..., 1:], zeros], axis=-1)
    east_going = (cosines > 0.0).astype(jnp.float32)[None, None, :, None]
    return east_going * (east_flux - behind) + (1.0 - east_going) * (ahead - east_flux)

def reference(energy, water_depth, wet_mask, vegetation, canopy, quad_offsets, quad_weights):
    wet_field = wet_mask.astype(jnp.float32)
    veg_field = vegetation.astype(jnp.float32)
    masked = wet_field[:, None, None, :] * energy
    radian_freq = 2.0 * math.pi * base_freq * jnp.power(freq_ratio, jnp.arange(FREQS, dtype=jnp.float32))
    group_speed, orbit_weight = physics(radian_freq, water_depth, DIRS)
    orbital = jnp.sqrt(lax.optimization_barrier(jnp.sum(orbit_weight * lax.optimization_barrier(jnp.sum(energy, axis=2)), axis=1)))
    full_step = SUBSTEPS * sub_step
    damping = 1.0 + full_step * canopy * veg_field * orbital
    padding = ((0, 0), (FH, FH), (0, 0), (0, 0))
    blocks = NY // CY

    def source_block(items):
        block_masked, block_damp = items
        transfer = interaction(jnp.pad(block_masked, padding), block_masked, quad_offsets, quad_weights)
        change = redistribute(jnp.pad(transfer, padding), transfer, quad_offsets, quad_weights)
        return (block_masked + full_step * change) / block_damp[:, None, None, :] - block_masked
    increment = lax.map(source_block, (masked.reshape(blocks, CY, FREQS, DIRS, NX), damping.reshape(blocks, CY, NX)))
    increment = increment.reshape(NY, FREQS, DIRS, NX)
    cosines, sines = angles_of(DIRS)
    wet_four = wet_field[:, None, None, :]

    def move_one(items):
        spectrum, speed = items
        spectrum = spectrum[:, None]
        speed = speed[:, None]
        east_speed = speed[:, :, None, :] * cosines[None, None, :, None]
        north_speed = speed[:, :, None, :] * sines[None, None, :, None]
        north_going = (sines > 0.0).astype(jnp.float32)[None, None, :, None]
        for substep in range(SUBSTEPS):
            east_flux = east_speed * spectrum
            north_flux = north_speed * spectrum
            zeros = jnp.zeros_like(north_flux[:1])
            below = jnp.concatenate([zeros, north_flux[:-1]], axis=0)
            above = jnp.concatenate([north_flux[1:], zeros], axis=0)
            along = north_going * (north_flux - below) + (1.0 - north_going) * (above - north_flux)
            spectrum = wet_four * (spectrum - sub_step / cell_size * (east_west(east_flux, cosines) + along))
        return spectrum[:, 0]
    moved = lax.map(move_one, (jnp.moveaxis(masked, 1, 0), jnp.moveaxis(group_speed, 1, 0)))
    moved = jnp.moveaxis(moved, 0, 1)
    return (wet_four * (moved + increment), orbital)
```

```python
import functools
import math

import jax
import jax.numpy as jnp
import numpy as np
from jax import lax
from jax.experimental import pallas as pl
from jax.experimental.pallas import tpu as pltpu
from jax.sharding import PartitionSpec as P

FH = 4
SUBSTEPS = 8


gravity = 9.81
base_freq = 0.03
freq_ratio = 1.05
cell_size = 20.0
sub_step = 2.0
coupling = 0.01
coef_plus = 0.4096
coef_minus = 3.1605
coef_both = 2.589


def padded(block, sides, width):
    for axis, dim in sides:
        count = lax.axis_size(axis)
        forward = [(i, i + 1) for i in range(count - 1)]
        backward = [(target, source) for source, target in forward]
        low = lax.ppermute(
            lax.slice_in_dim(block, block.shape[dim] - width, None, axis=dim), axis, forward
        )
        high = lax.ppermute(lax.slice_in_dim(block, 0, width, axis=dim), axis, backward)
        block = jnp.concatenate([low, block, high], axis=dim)
    return block


def physics(radian_freq, water_depth, dir_count):
    square = (radian_freq * radian_freq)[None, :, None]
    column = water_depth[:, None, :]
    depth_ratio = square * column / gravity
    depth_wave = depth_ratio / jnp.sqrt(jnp.tanh(depth_ratio))
    group_speed = (
        radian_freq[None, :, None]
        * column
        / depth_wave
        * (0.5 + depth_wave / jnp.sinh(2.0 * depth_wave))
    )
    orbit_weight = (
        square
        / jnp.sinh(depth_wave) ** 2
        * (radian_freq * (freq_ratio - 1.0))[None, :, None]
        * (2.0 * math.pi / dir_count)
    )
    return (group_speed, orbit_weight)


def angles_of(dir_count):
    angles = (jnp.arange(dir_count, dtype=jnp.float32) + 0.5) * (2.0 * math.pi / dir_count)
    return (jnp.cos(angles), jnp.sin(angles))


def shifted(doubled, freq_off, dir_off, count):
    dir_count = doubled.shape[2] // 2
    starts = (
        jnp.zeros((), jnp.int32),
        freq_off + FH,
        dir_off % dir_count,
        jnp.zeros((), jnp.int32),
    )
    return lax.dynamic_slice(
        doubled, starts, (doubled.shape[0], count, dir_count, doubled.shape[3])
    )


def interaction(extended, masked, quad_offsets, quad_weights):
    count = masked.shape[1]
    doubled = jnp.concatenate([extended, extended], axis=2)
    up_bins, down_bins, up_turn, down_turn = (
        quad_offsets[0],
        quad_offsets[1],
        quad_offsets[2],
        quad_offsets[3],
    )
    weight_up, weight_down = (quad_weights[0], quad_weights[1])
    upper = weight_up * shifted(doubled, up_bins, up_turn, count) + (1.0 - weight_up) * shifted(
        doubled, up_bins + 1, up_turn, count
    )
    lower = weight_down * shifted(doubled, -down_bins, -down_turn, count) + (
        1.0 - weight_down
    ) * shifted(doubled, -down_bins - 1, -down_turn, count)
    return coupling * (
        masked * masked * (coef_plus * upper + coef_minus * lower)
        - coef_both * masked * upper * lower
    )


def redistribute(extended, transfer, quad_offsets, quad_weights):
    count = transfer.shape[1]
    doubled = jnp.concatenate([extended, extended], axis=2)
    up_bins, down_bins, up_turn, down_turn = (
        quad_offsets[0],
        quad_offsets[1],
        quad_offsets[2],
        quad_offsets[3],
    )
    weight_up, weight_down = (quad_weights[0], quad_weights[1])
    gained = weight_up * shifted(doubled, -up_bins, -up_turn, count) + (1.0 - weight_up) * shifted(
        doubled, -up_bins - 1, -up_turn, count
    )
    gained = (
        gained
        + weight_down * shifted(doubled, down_bins, down_turn, count)
        + (1.0 - weight_down) * shifted(doubled, down_bins + 1, down_turn, count)
    )
    return gained - 2.0 * transfer


def east_west(east_flux, cosines):
    zeros = jnp.zeros_like(east_flux[..., :1])
    behind = jnp.concatenate([zeros, east_flux[..., :-1]], axis=-1)
    ahead = jnp.concatenate([east_flux[..., 1:], zeros], axis=-1)
    east_going = (cosines > 0.0).astype(jnp.float32)[None, None, :, None]
    return east_going * (east_flux - behind) + (1.0 - east_going) * (ahead - east_flux)


def plain_body(energy, water_depth, wet_mask, vegetation, canopy, quad_offsets, quad_weights):
    tile_rows, freq_count, dir_count, tile_cols = energy.shape
    wet_field = wet_mask.astype(jnp.float32)
    veg_field = vegetation.astype(jnp.float32)
    wet_four = wet_field[:, None, None, :]
    masked = wet_four * energy
    first_bin = lax.axis_index("freq") * freq_count
    bin_index = (first_bin + jnp.arange(freq_count, dtype=jnp.int32)).astype(jnp.float32)
    radian_freq = 2.0 * math.pi * base_freq * jnp.power(freq_ratio, bin_index)
    group_speed, orbit_weight = physics(radian_freq, water_depth, dir_count)
    partial_value = jnp.sum(orbit_weight * jnp.sum(energy, axis=2), axis=1)
    orbital = jnp.sqrt(lax.psum(partial_value, "freq"))
    full_step = SUBSTEPS * sub_step
    damping = 1.0 + full_step * canopy * veg_field * orbital
    extended = padded(masked, (("freq", 1),), FH)
    transfer = interaction(extended, masked, quad_offsets, quad_weights)
    spread = padded(transfer, (("freq", 1),), FH)
    change = redistribute(spread, transfer, quad_offsets, quad_weights)
    increment = (masked + full_step * change) / damping[:, None, None, :] - masked
    cosines, sines = angles_of(dir_count)
    step_ratio = sub_step / cell_size
    east_speed = group_speed[:, :, None, :] * cosines[None, None, :, None]
    north_speed = group_speed[:, :, None, :] * sines[None, None, :, None]
    north_going = (sines > 0.0).astype(jnp.float32)[None, None, :, None]
    spectrum = masked
    for substep in range(SUBSTEPS):
        east_flux = east_speed * spectrum
        north_flux = north_speed * spectrum
        rimmed = padded(north_flux, (("geo", 0),), 1)
        below = rimmed[:-2]
        above = rimmed[2:]
        along = north_going * (north_flux - below) + (1.0 - north_going) * (above - north_flux)
        spectrum = wet_four * (spectrum - step_ratio * (east_west(east_flux, cosines) + along))
    return (wet_four * (spectrum + increment), orbital)


MESH = pl.DeviceIdType.MESH
ROWS = 4
REACH = 8
PART = 3


def sinh_of(x):
    square = x * x
    series = 1.0 + square / 210.0
    for term in (156.0, 110.0, 72.0, 42.0, 20.0, 6.0):
        series = 1.0 + square / term * series
    wide = jnp.exp(x)
    return jnp.where(x < 1.7, x * series, 0.5 * (wide - 1.0 / wide))


def tanh_of(x):
    low = sinh_of(jnp.minimum(x, 1.0))
    fall = jnp.exp(-2.0 * x)
    return jnp.where(x < 1.0, low / jnp.sqrt(1.0 + low * low), (1.0 - fall) / (1.0 + fall))


def kernel(
    groups,
    tiles,
    dirs,
    quad_offsets,
    quad_weights,
    coefs,
    energy,
    radian,
    depth,
    wet_mask,
    vegetation,
    canopy,
    out,
    orbital,
    ext,
    quads,
    spec,
    incr,
    inbox,
    outbox,
    fringe,
    speed,
    wet,
    drag,
    part_mine,
    part_theirs,
    send_sem,
    recv_sem,
    fringe_sems,
    part_sems,
):
    bins = energy.shape[2]
    quarter = dirs // 4
    parts = quarter // PART
    mine = lax.axis_index("freq")
    tile = lax.axis_index("geo")
    has_below = tile > 0
    has_above = tile < tiles - 1
    below_id = jnp.maximum(tile - 1, 0)
    above_id = jnp.minimum(tile + 1, tiles - 1)

    barrier = pltpu.get_barrier_semaphore()
    pl.semaphore_signal(barrier, inc=1, device_id=(1 - mine, tile), device_id_type=MESH)

    @pl.when(has_below)
    def _():
        pl.semaphore_signal(barrier, inc=1, device_id=(mine, below_id), device_id_type=MESH)

    @pl.when(has_above)
    def _():
        pl.semaphore_signal(barrier, inc=1, device_id=(mine, above_id), device_id_type=MESH)

    first = pl.multiple_of(mine * bins, 8)
    freq = radian[pl.ds(first, bins), :]
    square = freq * freq
    for row in range(ROWS):
        column = jnp.broadcast_to(depth[row : row + 1, :], (bins, 128))
        ratio = square * column / gravity
        wave = ratio / jnp.sqrt(tanh_of(ratio))
        speed[row] = (sub_step / cell_size) * (
            freq * column / wave * (0.5 + wave / sinh_of(2.0 * wave))
        )
        wet[row] = jnp.broadcast_to(wet_mask[row : row + 1, :].astype(jnp.float32), (bins, 128))

    def edge(step, q, k):
        first_dir = q * quarter + k * PART
        north = q < 2
        return pltpu.make_async_remote_copy(
            src_ref=outbox.at[step, pl.ds(first_dir, PART)],
            dst_ref=inbox.at[step, pl.ds(first_dir, PART)],
            send_sem=send_sem.at[step, q, k],
            recv_sem=recv_sem.at[step, q, k],
            device_id=(mine, above_id if north else below_id),
            device_id_type=MESH,
        )

    def sends(q):
        return has_above if q < 2 else has_below

    def receives(q):
        return has_below if q < 2 else has_above

    waits = 1 + has_below.astype(jnp.int32) + has_above.astype(jnp.int32)
    pl.semaphore_wait(barrier, waits)

    def first_edges(k, carry):
        for q in (0, 2, 1, 3):
            row = ROWS - 1 if q < 2 else 0
            for d in range(PART):
                j = q * quarter + k * PART + d
                outbox[0, j] = speed[row] * (wet[row] * energy[j, row])

            @pl.when(sends(q))
            def _():
                edge(0, q, k).start()

        return carry

    lax.fori_loop(0, parts, first_edges, 0)

    fringe_copy = pltpu.make_async_remote_copy(
        src_ref=energy.at[:, :, pl.ds(pl.multiple_of((1 - mine) * (bins - REACH), 8), REACH), :],
        dst_ref=fringe,
        send_sem=fringe_sems.at[0],
        recv_sem=fringe_sems.at[1],
        device_id=(1 - mine, tile),
        device_id_type=MESH,
    )
    fringe_copy.start()

    @pl.when(jnp.logical_not(has_below))
    def _():
        def clear(step, carry):
            inbox[step, pl.ds(0, 2 * quarter)] = jnp.zeros((2 * quarter, bins, 128), jnp.float32)
            return carry

        lax.fori_loop(0, SUBSTEPS, clear, 0)

    @pl.when(jnp.logical_not(has_above))
    def _():
        def clear(step, carry):
            inbox[step, pl.ds(2 * quarter, 2 * quarter)] = jnp.zeros(
                (2 * quarter, bins, 128), jnp.float32
            )
            return carry

        lax.fori_loop(0, SUBSTEPS, clear, 0)

    empty = pl.multiple_of(mine * (REACH + bins), 8)
    taken = pl.multiple_of((1 - mine) * (REACH + bins), 8)

    def fill(j, totals):
        sums = []
        for row in range(ROWS):
            raw = energy[j, row]
            wetted = wet[row] * raw
            spec[j, row] = wetted
            ext[j, row, REACH : REACH + bins, :] = wetted
            ext[j, row, pl.ds(empty, REACH), :] = jnp.zeros((REACH, 128), jnp.float32)
            sums.append(totals[row] + raw)
        return tuple(sums)

    totals = lax.fori_loop(
        0, dirs, fill, tuple(jnp.zeros((bins, 128), jnp.float32) for _ in range(ROWS))
    )
    for row in range(ROWS):
        column = jnp.broadcast_to(depth[row : row + 1, :], (bins, 128))
        ratio = square * column / gravity
        wave = ratio / jnp.sqrt(tanh_of(ratio))
        steep = sinh_of(wave)
        weight = (
            square / (steep * steep) * (freq * (freq_ratio - 1.0)) * (2.0 * math.pi / dirs)
        )
        part_mine[row] = jnp.broadcast_to(
            jnp.sum(weight * totals[row], axis=0, keepdims=True), (8, 128)
        )
    part_copy = pltpu.make_async_remote_copy(
        src_ref=part_mine,
        dst_ref=part_theirs,
        send_sem=part_sems.at[0],
        recv_sem=part_sems.at[1],
        device_id=(1 - mine, tile),
        device_id_type=MESH,
    )
    part_copy.start()

    lane = lax.broadcasted_iota(jnp.int32, (bins, 128), 1)

    def move(step, q, k, last):
        east = q in (0, 3)
        north = q < 2
        inside = (lane != (0 if east else 127)).astype(jnp.float32)
        order = range(ROWS) if north else range(ROWS - 1, -1, -1)
        for d in range(PART):
            j = q * quarter + k * PART + d
            across, along = coefs[0, j], coefs[1, j]
            both = across + along
            sideways = across * inside
            before = inbox[step, j]
            for row in order:
                held = spec[j, row]
                flux = speed[row] * held
                beside = pltpu.roll(flux, 1 if east else 127, 1)
                fresh = wet[row] * (held - both * flux + sideways * beside + along * before)
                before = flux
                if last:
                    out[j, row] = fresh + wet[row] * incr[j, row]
                else:
                    spec[j, row] = fresh
            if not last:
                outbox[step + 1, j] = speed[row] * fresh

    def substep(step, last=False):
        def piece(k, carry):
            for q in (0, 2, 1, 3):

                @pl.when(receives(q))
                def _():
                    edge(step, q, k).wait_recv()

                move(step, q, k, last)
                if not last:

                    @pl.when(sends(q))
                    def _():
                        edge(step + 1, q, k).start()

            return carry

        lax.fori_loop(0, parts, piece, 0)

    def plain_step(step, carry):
        substep(step)
        return carry

    lax.fori_loop(0, 3, plain_step, 0)

    part_copy.wait()
    fringe_copy.wait()

    for row in range(ROWS):
        total = jnp.sqrt(part_mine[row] + part_theirs[row])
        orbital[row : row + 1, :] = total[0:1, :]
        leaves = vegetation[row : row + 1, :].astype(jnp.float32) * canopy[row : row + 1, :]
        damping = 1.0 + (SUBSTEPS * sub_step) * leaves * total[0:1, :]
        drag[row] = jnp.broadcast_to(1.0 / damping, (bins, 128))

    def take(j, carry):
        for row in range(ROWS):
            ext[j, row, pl.ds(taken, REACH), :] = wet[row, 0:REACH, :] * fringe[j, row]
        return carry

    lax.fori_loop(0, dirs, take, 0)

    up_bins, up_turn, down_turn = quad_offsets[0], quad_offsets[2], quad_offsets[3]
    weight_up, weight_down = quad_weights[0], quad_weights[1]
    rest_up, rest_down = 1.0 - weight_up, 1.0 - weight_down
    half = REACH // 2
    span = bins + REACH

    def turned(j, turn):
        j = j + turn
        j = jnp.where(j >= dirs, j - dirs, j)
        return jnp.where(j < 0, j + dirs, j)

    def couple(j, carry):
        high, low = turned(j, up_turn), turned(j, -down_turn)
        for row in range(ROWS):
            here = ext[j, row, half : half + span, :]
            upper = (
                weight_up * ext[high, row, pl.ds(half + up_bins, span), :]
                + rest_up * ext[high, row, pl.ds(half + up_bins + 1, span), :]
            )
            lower = (
                weight_down * ext[low, row, half - 3 : half - 3 + span, :]
                + rest_down * ext[low, row, half - 4 : half - 4 + span, :]
            )
            quads[j, row] = (coupling * here) * (
                here * (coef_plus * upper + coef_minus * lower) - coef_both * (upper * lower)
            )
        return carry

    def spread(j, carry):
        back, ahead = turned(j, -up_turn), turned(j, down_turn)
        for row in range(ROWS):
            change = (
                weight_up * quads[back, row, pl.ds(half - up_bins, bins), :]
                + rest_up * quads[back, row, pl.ds(half - up_bins - 1, bins), :]
                + weight_down * quads[ahead, row, half + 3 : half + 3 + bins, :]
                + rest_down * quads[ahead, row, half + 4 : half + 4 + bins, :]
                - 2.0 * quads[j, row, half : half + bins, :]
            )
            wetted = ext[j, row, REACH : REACH + bins, :]
            incr[j, row] = (wetted + (SUBSTEPS * sub_step) * change) * drag[row] - wetted
        return carry

    def couple_step(step, carry):
        substep(step)
        lax.fori_loop((step - 3) * (dirs // 2), (step - 2) * (dirs // 2), couple, 0)
        return carry

    def spread_step(step, carry):
        substep(step)
        lax.fori_loop((step - 5) * (dirs // 2), (step - 4) * (dirs // 2), spread, 0)
        return carry

    lax.fori_loop(3, 5, couple_step, 0)
    lax.fori_loop(5, 7, spread_step, 0)
    substep(SUBSTEPS - 1, last=True)

    def drain(step, carry):
        def piece(k, inner):
            for q in range(4):

                @pl.when(sends(q))
                def _():
                    edge(step, q, k).wait_send()

            return inner

        return lax.fori_loop(0, parts, piece, carry)

    lax.fori_loop(0, SUBSTEPS, drain, 0)


def kernel_body(groups, tiles, energy, water_depth, wet_mask, vegetation, canopy, offsets, weights):
    rows, bins, dirs, cols = energy.shape
    angles = (np.arange(dirs, dtype=np.float32) + np.float32(0.5)) * np.float32(
        2.0 * math.pi / dirs
    )
    coefs = np.abs(np.stack([np.cos(angles), np.sin(angles)])).astype(np.float32)
    radian = 2.0 * math.pi * base_freq * freq_ratio ** np.arange(groups * bins)
    radian = np.broadcast_to(radian.astype(np.float32)[:, None], (groups * bins, cols))
    vmem = pl.BlockSpec(memory_space=pltpu.VMEM)
    smem = pl.BlockSpec(memory_space=pltpu.SMEM)
    f32 = jnp.float32
    parts = dirs // 4 // PART
    moved, orbital = pl.pallas_call(
        functools.partial(kernel, groups, tiles, dirs),
        out_shape=(
            jax.ShapeDtypeStruct((dirs, rows, bins, cols), f32),
            jax.ShapeDtypeStruct((rows, cols), f32),
        ),
        in_specs=[smem] * 3 + [vmem] * 6,
        out_specs=(vmem, vmem),
        scratch_shapes=[
            pltpu.VMEM((dirs, rows, bins + 2 * REACH, cols), f32),
            pltpu.VMEM((dirs, rows, bins + REACH, cols), f32),
            pltpu.VMEM((dirs, rows, bins, cols), f32),
            pltpu.VMEM((dirs, rows, bins, cols), f32),
            pltpu.VMEM((SUBSTEPS, dirs, bins, cols), f32),
            pltpu.VMEM((SUBSTEPS, dirs, bins, cols), f32),
            pltpu.VMEM((dirs, rows, REACH, cols), f32),
            pltpu.VMEM((rows, bins, cols), f32),
            pltpu.VMEM((rows, bins, cols), f32),
            pltpu.VMEM((rows, bins, cols), f32),
            pltpu.VMEM((rows, 8, cols), f32),
            pltpu.VMEM((rows, 8, cols), f32),
            pltpu.SemaphoreType.DMA((SUBSTEPS, 4, parts)),
            pltpu.SemaphoreType.DMA((SUBSTEPS, 4, parts)),
            pltpu.SemaphoreType.DMA((2,)),
            pltpu.SemaphoreType.DMA((2,)),
        ],
        compiler_params=pltpu.CompilerParams(
            collective_id=0, has_side_effects=True, vmem_limit_bytes=48 * 1024 * 1024
        ),
    )(
        offsets,
        weights,
        jnp.asarray(coefs),
        jnp.transpose(energy, (2, 0, 1, 3)),
        jnp.asarray(radian),
        water_depth,
        wet_mask,
        vegetation,
        canopy,
    )
    return jnp.transpose(moved, (1, 2, 0, 3)), orbital


def body(groups, tiles, energy, *rest):
    rows, bins, dirs, cols = energy.shape
    if groups == 2 and rows == ROWS and bins % 8 == 0 and dirs % (4 * PART) == 0 and cols == 128:
        return kernel_body(groups, tiles, energy, *rest)
    return plain_body(energy, *rest)


def solution(mesh):
    placed = (
        P("geo", "freq", None, None),
        P("geo", None),
        P("geo", None),
        P("geo", None),
        P("geo", None),
        P(),
        P(),
    )
    return jax.shard_map(
        functools.partial(body, mesh.shape["freq"], mesh.shape["geo"]),
        mesh=mesh,
        in_specs=placed,
        out_specs=(P("geo", "freq", None, None), P("geo", None)),
        check_vma=False,
    )
```

```python
import functools
import math

import jax
import jax.numpy as jnp
import numpy as np
from jax import lax
from jax.experimental import pallas as pl
from jax.experimental.pallas import tpu as pltpu
from jax.sharding import PartitionSpec as P

FH = 4
SUBSTEPS = 8


gravity = 9.81
base_freq = 0.03
freq_ratio = 1.05
cell_size = 20.0
sub_step = 2.0
coupling = 0.01
coef_plus = 0.4096
coef_minus = 3.1605
coef_both = 2.589


def padded(block, sides, width):
    for axis, dim in sides:
        count = lax.axis_size(axis)
        forward = [(i, i + 1) for i in range(count - 1)]
        backward = [(target, source) for source, target in forward]
        low = lax.ppermute(
            lax.slice_in_dim(block, block.shape[dim] - width, None, axis=dim), axis, forward
        )
        high = lax.ppermute(lax.slice_in_dim(block, 0, width, axis=dim), axis, backward)
        block = jnp.concatenate([low, block, high], axis=dim)
    return block


def physics(radian_freq, water_depth, dir_count):
    square = (radian_freq * radian_freq)[None, :, None]
    column = water_depth[:, None, :]
    depth_ratio = square * column / gravity
    depth_wave = depth_ratio / jnp.sqrt(jnp.tanh(depth_ratio))
    group_speed = (
        radian_freq[None, :, None]
        * column
        / depth_wave
        * (0.5 + depth_wave / jnp.sinh(2.0 * depth_wave))
    )
    orbit_weight = (
        square
        / jnp.sinh(depth_wave) ** 2
        * (radian_freq * (freq_ratio - 1.0))[None, :, None]
        * (2.0 * math.pi / dir_count)
    )
    return (group_speed, orbit_weight)


def angles_of(dir_count):
    angles = (jnp.arange(dir_count, dtype=jnp.float32) + 0.5) * (2.0 * math.pi / dir_count)
    return (jnp.cos(angles), jnp.sin(angles))


def shifted(doubled, freq_off, dir_off, count):
    dir_count = doubled.shape[2] // 2
    starts = (
        jnp.zeros((), jnp.int32),
        freq_off + FH,
        dir_off % dir_count,
        jnp.zeros((), jnp.int32),
    )
    return lax.dynamic_slice(
        doubled, starts, (doubled.shape[0], count, dir_count, doubled.shape[3])
    )


def interaction(extended, masked, quad_offsets, quad_weights):
    count = masked.shape[1]
    doubled = jnp.concatenate([extended, extended], axis=2)
    up_bins, down_bins, up_turn, down_turn = (
        quad_offsets[0],
        quad_offsets[1],
        quad_offsets[2],
        quad_offsets[3],
    )
    weight_up, weight_down = (quad_weights[0], quad_weights[1])
    upper = weight_up * shifted(doubled, up_bins, up_turn, count) + (1.0 - weight_up) * shifted(
        doubled, up_bins + 1, up_turn, count
    )
    lower = weight_down * shifted(doubled, -down_bins, -down_turn, count) + (
        1.0 - weight_down
    ) * shifted(doubled, -down_bins - 1, -down_turn, count)
    return coupling * (
        masked * masked * (coef_plus * upper + coef_minus * lower)
        - coef_both * masked * upper * lower
    )


def redistribute(extended, transfer, quad_offsets, quad_weights):
    count = transfer.shape[1]
    doubled = jnp.concatenate([extended, extended], axis=2)
    up_bins, down_bins, up_turn, down_turn = (
        quad_offsets[0],
        quad_offsets[1],
        quad_offsets[2],
        quad_offsets[3],
    )
    weight_up, weight_down = (quad_weights[0], quad_weights[1])
    gained = weight_up * shifted(doubled, -up_bins, -up_turn, count) + (1.0 - weight_up) * shifted(
        doubled, -up_bins - 1, -up_turn, count
    )
    gained = (
        gained
        + weight_down * shifted(doubled, down_bins, down_turn, count)
        + (1.0 - weight_down) * shifted(doubled, down_bins + 1, down_turn, count)
    )
    return gained - 2.0 * transfer


def east_west(east_flux, cosines):
    zeros = jnp.zeros_like(east_flux[..., :1])
    behind = jnp.concatenate([zeros, east_flux[..., :-1]], axis=-1)
    ahead = jnp.concatenate([east_flux[..., 1:], zeros], axis=-1)
    east_going = (cosines > 0.0).astype(jnp.float32)[None, None, :, None]
    return east_going * (east_flux - behind) + (1.0 - east_going) * (ahead - east_flux)


def plain_body(energy, water_depth, wet_mask, vegetation, canopy, quad_offsets, quad_weights):
    tile_rows, freq_count, dir_count, tile_cols = energy.shape
    wet_field = wet_mask.astype(jnp.float32)
    veg_field = vegetation.astype(jnp.float32)
    wet_four = wet_field[:, None, None, :]
    masked = wet_four * energy
    first_bin = lax.axis_index("freq") * freq_count
    bin_index = (first_bin + jnp.arange(freq_count, dtype=jnp.int32)).astype(jnp.float32)
    radian_freq = 2.0 * math.pi * base_freq * jnp.power(freq_ratio, bin_index)
    group_speed, orbit_weight = physics(radian_freq, water_depth, dir_count)
    partial_value = jnp.sum(orbit_weight * jnp.sum(energy, axis=2), axis=1)
    orbital = jnp.sqrt(lax.psum(partial_value, "freq"))
    full_step = SUBSTEPS * sub_step
    damping = 1.0 + full_step * canopy * veg_field * orbital
    extended = padded(masked, (("freq", 1),), FH)
    transfer = interaction(extended, masked, quad_offsets, quad_weights)
    spread = padded(transfer, (("freq", 1),), FH)
    change = redistribute(spread, transfer, quad_offsets, quad_weights)
    increment = (masked + full_step * change) / damping[:, None, None, :] - masked
    cosines, sines = angles_of(dir_count)
    step_ratio = sub_step / cell_size
    east_speed = group_speed[:, :, None, :] * cosines[None, None, :, None]
    north_speed = group_speed[:, :, None, :] * sines[None, None, :, None]
    north_going = (sines > 0.0).astype(jnp.float32)[None, None, :, None]
    spectrum = masked
    for substep in range(SUBSTEPS):
        east_flux = east_speed * spectrum
        north_flux = north_speed * spectrum
        rimmed = padded(north_flux, (("geo", 0),), 1)
        below = rimmed[:-2]
        above = rimmed[2:]
        along = north_going * (north_flux - below) + (1.0 - north_going) * (above - north_flux)
        spectrum = wet_four * (spectrum - step_ratio * (east_west(east_flux, cosines) + along))
    return (wet_four * (spectrum + increment), orbital)


MESH = pl.DeviceIdType.MESH
ROWS = 4
REACH = 8
PART = 3


def sinh_of(x):
    square = x * x
    series = 1.0 + square / 210.0
    for term in (156.0, 110.0, 72.0, 42.0, 20.0, 6.0):
        series = 1.0 + square / term * series
    wide = jnp.exp(x)
    return jnp.where(x < 1.7, x * series, 0.5 * (wide - 1.0 / wide))


def tanh_of(x):
    low = sinh_of(jnp.minimum(x, 1.0))
    fall = jnp.exp(-2.0 * x)
    return jnp.where(x < 1.0, low / jnp.sqrt(1.0 + low * low), (1.0 - fall) / (1.0 + fall))


def kernel(
    groups,
    tiles,
    dirs,
    quad_offsets,
    quad_weights,
    coefs,
    energy,
    radian,
    depth,
    wet_mask,
    vegetation,
    canopy,
    out,
    orbital,
    loaded,
    stored,
    ext,
    quads,
    spec,
    incr,
    inbox,
    outbox,
    speed,
    wet,
    drag,
    part_mine,
    part_theirs,
    send_sem,
    recv_sem,
    fringe_sems,
    part_sems,
    load_sem,
    store_sem,
):
    bins = energy.shape[1]
    quarter = dirs // 4
    parts = quarter // PART
    mine = lax.axis_index("freq")
    tile = lax.axis_index("geo")
    has_below = tile > 0
    has_above = tile < tiles - 1
    below_id = jnp.maximum(tile - 1, 0)
    above_id = jnp.minimum(tile + 1, tiles - 1)

    def load(row):
        return pltpu.make_async_copy(energy.at[row], loaded.at[row], load_sem.at[row])

    for row in (ROWS - 1, 0, *range(1, ROWS - 1)):
        load(row).start()

    barrier = pltpu.get_barrier_semaphore()
    pl.semaphore_signal(barrier, inc=1, device_id=(1 - mine, tile), device_id_type=MESH)

    @pl.when(has_below)
    def _():
        pl.semaphore_signal(barrier, inc=1, device_id=(mine, below_id), device_id_type=MESH)

    @pl.when(has_above)
    def _():
        pl.semaphore_signal(barrier, inc=1, device_id=(mine, above_id), device_id_type=MESH)

    first = pl.multiple_of(mine * bins, 8)
    freq = radian[pl.ds(first, bins), :]
    square = freq * freq
    for row in range(ROWS):
        column = jnp.broadcast_to(depth[row : row + 1, :], (bins, 128))
        ratio = square * column / gravity
        wave = ratio / jnp.sqrt(tanh_of(ratio))
        speed[row] = (sub_step / cell_size) * (
            freq * column / wave * (0.5 + wave / sinh_of(2.0 * wave))
        )
        wet[row] = jnp.broadcast_to(wet_mask[row : row + 1, :].astype(jnp.float32), (bins, 128))

    def edge(step, q, k):
        first_dir = q * quarter + k * PART
        north = q < 2
        return pltpu.make_async_remote_copy(
            src_ref=outbox.at[step, pl.ds(first_dir, PART)],
            dst_ref=inbox.at[step, pl.ds(first_dir, PART)],
            send_sem=send_sem.at[step, q, k],
            recv_sem=recv_sem.at[step, q, k],
            device_id=(mine, above_id if north else below_id),
            device_id_type=MESH,
        )

    def sends(q):
        return has_above if q < 2 else has_below

    def receives(q):
        return has_below if q < 2 else has_above


    empty = pl.multiple_of(mine * (REACH + bins), 8)
    leaving = pl.multiple_of(REACH + (1 - mine) * (bins - REACH), 8)

    def fill(row):
        load(row).wait()
        total = jnp.zeros((bins, 128), jnp.float32)
        for base in range(0, dirs, 8):
            count = min(8, dirs - base)
            raw = jnp.swapaxes(loaded[row, :, base : base + count, :], 0, 1)
            total = total + jnp.sum(raw, axis=0)
            wetted = wet[row][None] * raw
            spec[base : base + count, row] = wetted
            ext[base : base + count, row, REACH : REACH + bins, :] = wetted
            ext[base : base + count, row, pl.ds(empty, REACH), :] = jnp.zeros(
                (count, REACH, 128), jnp.float32
            )
        return total

    def first_edges(k, carry):
        for q in (0, 2, 1, 3):
            row = ROWS - 1 if q < 2 else 0
            for d in range(PART):
                j = q * quarter + k * PART + d
                outbox[0, j] = speed[row] * spec[j, row]

            @pl.when(sends(q))
            def _():
                edge(0, q, k).start()

        return carry

    totals = {row: fill(row) for row in (ROWS - 1, 0)}
    waits = 1 + has_below.astype(jnp.int32) + has_above.astype(jnp.int32)
    pl.semaphore_wait(barrier, waits)
    lax.fori_loop(0, parts, first_edges, 0)
    for row in range(1, ROWS - 1):
        totals[row] = fill(row)

    pieces = 3 * parts
    width = dirs // pieces

    def fringe_copy(piece):
        some = pl.ds(piece * width, width)
        return pltpu.make_async_remote_copy(
            src_ref=ext.at[some, :, pl.ds(leaving, REACH), :],
            dst_ref=ext.at[some, :, pl.ds(empty, REACH), :],
            send_sem=fringe_sems.at[0, piece],
            recv_sem=fringe_sems.at[1, piece],
            device_id=(1 - mine, tile),
            device_id_type=MESH,
        )

    @pl.when(jnp.logical_not(has_below))
    def _():
        def clear(step, carry):
            inbox[step, pl.ds(0, 2 * quarter)] = jnp.zeros((2 * quarter, bins, 128), jnp.float32)
            return carry

        lax.fori_loop(0, SUBSTEPS, clear, 0)

    @pl.when(jnp.logical_not(has_above))
    def _():
        def clear(step, carry):
            inbox[step, pl.ds(2 * quarter, 2 * quarter)] = jnp.zeros(
                (2 * quarter, bins, 128), jnp.float32
            )
            return carry

        lax.fori_loop(0, SUBSTEPS, clear, 0)

    for row in range(ROWS):
        column = jnp.broadcast_to(depth[row : row + 1, :], (bins, 128))
        ratio = square * column / gravity
        wave = ratio / jnp.sqrt(tanh_of(ratio))
        steep = sinh_of(wave)
        weight = (
            square / (steep * steep) * (freq * (freq_ratio - 1.0)) * (2.0 * math.pi / dirs)
        )
        part_mine[row] = jnp.broadcast_to(
            jnp.sum(weight * totals[row], axis=0, keepdims=True), (8, 128)
        )
    part_copy = pltpu.make_async_remote_copy(
        src_ref=part_mine,
        dst_ref=part_theirs,
        send_sem=part_sems.at[0],
        recv_sem=part_sems.at[1],
        device_id=(1 - mine, tile),
        device_id_type=MESH,
    )
    part_copy.start()

    lane = lax.broadcasted_iota(jnp.int32, (bins, 128), 1)

    def move(step, q, k, last):
        east = q in (0, 3)
        north = q < 2
        inside = (lane != (0 if east else 127)).astype(jnp.float32)
        order = range(ROWS) if north else range(ROWS - 1, -1, -1)
        for d in range(PART):
            j = q * quarter + k * PART + d
            across, along = coefs[0, j], coefs[1, j]
            both = across + along
            sideways = across * inside
            before = inbox[step, j]
            for row in order:
                held = spec[j, row]
                flux = speed[row] * held
                beside = pltpu.roll(flux, 1 if east else 127, 1)
                fresh = wet[row] * (held - both * flux + sideways * beside + along * before)
                before = flux
                if last:
                    spec[j, row] = fresh + wet[row] * incr[j, row]
                else:
                    spec[j, row] = fresh
            if not last:
                outbox[step + 1, j] = speed[row] * fresh

    def substep(step, extra=None, last=False):
        for near, far in ((0, 2), (1, 3)):

            def piece(k, carry, near=near, far=far):
                for q in (near, far):

                    @pl.when(receives(q))
                    def _():
                        edge(step, q, k).wait_recv()

                    move(step, q, k, last)
                    if not last:

                        @pl.when(sends(q))
                        def _():
                            edge(step + 1, q, k).start()

                if extra is not None:
                    extra((near % 2) * parts + k)
                return carry

            lax.fori_loop(0, parts, piece, 0)

    def early_step(step, carry):
        def extra(n):
            @pl.when(n < parts)
            def _():
                fringe_copy(step * parts + n).start()

        substep(step, extra)
        return carry

    lax.fori_loop(0, 3, early_step, 0)
    substep(3)

    part_copy.wait()

    def fringe_wait(piece, carry):
        fringe_copy(piece).wait()
        return carry

    lax.fori_loop(0, pieces, fringe_wait, 0)

    for row in range(ROWS):
        total = jnp.sqrt(part_mine[row] + part_theirs[row])
        orbital[row : row + 1, :] = total[0:1, :]
        leaves = vegetation[row : row + 1, :].astype(jnp.float32) * canopy[row : row + 1, :]
        damping = 1.0 + (SUBSTEPS * sub_step) * leaves * total[0:1, :]
        drag[row] = jnp.broadcast_to(1.0 / damping, (bins, 128))

    up_bins, up_turn, down_turn = quad_offsets[0], quad_offsets[2], quad_offsets[3]
    weight_up, weight_down = quad_weights[0], quad_weights[1]
    rest_up, rest_down = 1.0 - weight_up, 1.0 - weight_down
    half = REACH // 2
    span = bins + REACH

    def turned(j, turn):
        j = j + turn
        j = jnp.where(j >= dirs, j - dirs, j)
        return jnp.where(j < 0, j + dirs, j)

    def couple(j, carry):
        high, low = turned(j, up_turn), turned(j, -down_turn)
        for row in range(ROWS):
            here = ext[j, row, half : half + span, :]
            upper = (
                weight_up * ext[high, row, pl.ds(half + up_bins, span), :]
                + rest_up * ext[high, row, pl.ds(half + up_bins + 1, span), :]
            )
            lower = (
                weight_down * ext[low, row, half - 3 : half - 3 + span, :]
                + rest_down * ext[low, row, half - 4 : half - 4 + span, :]
            )
            quads[j, row] = (coupling * here) * (
                here * (coef_plus * upper + coef_minus * lower) - coef_both * (upper * lower)
            )
        return carry

    def spread(j, carry):
        back, ahead = turned(j, -up_turn), turned(j, down_turn)
        for row in range(ROWS):
            change = (
                weight_up * quads[back, row, pl.ds(half - up_bins, bins), :]
                + rest_up * quads[back, row, pl.ds(half - up_bins - 1, bins), :]
                + weight_down * quads[ahead, row, half + 3 : half + 3 + bins, :]
                + rest_down * quads[ahead, row, half + 4 : half + 4 + bins, :]
                - 2.0 * quads[j, row, half : half + bins, :]
            )
            wetted = ext[j, row, REACH : REACH + bins, :]
            incr[j, row] = (wetted + (SUBSTEPS * sub_step) * change) * drag[row] - wetted
        return carry

    def couple_step(step, carry):
        share = dirs // (4 * parts)

        def extra(n):
            first_dir = ((step - 4) * 2 * parts + n) * share
            lax.fori_loop(first_dir, first_dir + share, couple, 0)

        substep(step, extra)
        return carry

    def spread_some(n):
        share = dirs // (2 * parts)
        lax.fori_loop(n * share, (n + 1) * share, spread, 0)

    lax.fori_loop(4, 6, couple_step, 0)
    substep(SUBSTEPS - 2, spread_some)
    substep(SUBSTEPS - 1, last=True)

    def store(row):
        return pltpu.make_async_copy(stored.at[row], out.at[row], store_sem.at[row])

    for row in range(ROWS):
        for base in range(0, dirs, 8):
            count = min(8, dirs - base)
            stored[row, :, base : base + count, :] = jnp.swapaxes(
                spec[base : base + count, row], 0, 1
            )
        store(row).start()

    def drain(step, carry):
        def piece(k, inner):
            for q in range(4):

                @pl.when(sends(q))
                def _():
                    edge(step, q, k).wait_send()

            return inner

        return lax.fori_loop(0, parts, piece, carry)

    lax.fori_loop(0, SUBSTEPS, drain, 0)
    for row in range(ROWS):
        store(row).wait()


def kernel_body(groups, tiles, energy, water_depth, wet_mask, vegetation, canopy, offsets, weights):
    rows, bins, dirs, cols = energy.shape
    angles = (np.arange(dirs, dtype=np.float32) + np.float32(0.5)) * np.float32(
        2.0 * math.pi / dirs
    )
    coefs = np.abs(np.stack([np.cos(angles), np.sin(angles)])).astype(np.float32)
    radian = 2.0 * math.pi * base_freq * freq_ratio ** np.arange(groups * bins)
    radian = np.broadcast_to(radian.astype(np.float32)[:, None], (groups * bins, cols))
    vmem = pl.BlockSpec(memory_space=pltpu.VMEM)
    smem = pl.BlockSpec(memory_space=pltpu.SMEM)
    f32 = jnp.float32
    parts = dirs // 4 // PART
    moved, orbital = pl.pallas_call(
        functools.partial(kernel, groups, tiles, dirs),
        out_shape=(
            jax.ShapeDtypeStruct((rows, bins, dirs, cols), f32),
            jax.ShapeDtypeStruct((rows, cols), f32),
        ),
        in_specs=[smem] * 3 + [pl.BlockSpec(memory_space=pl.ANY)] + [vmem] * 5,
        out_specs=(pl.BlockSpec(memory_space=pl.ANY), vmem),
        scratch_shapes=[
            pltpu.VMEM((rows, bins, dirs, cols), f32),
            pltpu.VMEM((rows, bins, dirs, cols), f32),
            pltpu.VMEM((dirs, rows, bins + 2 * REACH, cols), f32),
            pltpu.VMEM((dirs, rows, bins + REACH, cols), f32),
            pltpu.VMEM((dirs, rows, bins, cols), f32),
            pltpu.VMEM((dirs, rows, bins, cols), f32),
            pltpu.VMEM((SUBSTEPS, dirs, bins, cols), f32),
            pltpu.VMEM((SUBSTEPS, dirs, bins, cols), f32),
            pltpu.VMEM((rows, bins, cols), f32),
            pltpu.VMEM((rows, bins, cols), f32),
            pltpu.VMEM((rows, bins, cols), f32),
            pltpu.VMEM((rows, 8, cols), f32),
            pltpu.VMEM((rows, 8, cols), f32),
            pltpu.SemaphoreType.DMA((SUBSTEPS, 4, parts)),
            pltpu.SemaphoreType.DMA((SUBSTEPS, 4, parts)),
            pltpu.SemaphoreType.DMA((2, 3 * parts)),
            pltpu.SemaphoreType.DMA((2,)),
            pltpu.SemaphoreType.DMA((rows,)),
            pltpu.SemaphoreType.DMA((rows,)),
        ],
        compiler_params=pltpu.CompilerParams(
            collective_id=0, has_side_effects=True, vmem_limit_bytes=48 * 1024 * 1024
        ),
    )(
        offsets,
        weights,
        jnp.asarray(coefs),
        energy,
        jnp.asarray(radian),
        water_depth,
        wet_mask,
        vegetation,
        canopy,
    )
    return moved, orbital


def body(groups, tiles, energy, *rest):
    rows, bins, dirs, cols = energy.shape
    if groups == 2 and rows == ROWS and bins % 8 == 0 and dirs % (4 * PART) == 0 and cols == 128:
        return kernel_body(groups, tiles, energy, *rest)
    return plain_body(energy, *rest)


def solution(mesh):
    placed = (
        P("geo", "freq", None, None),
        P("geo", None),
        P("geo", None),
        P("geo", None),
        P("geo", None),
        P(),
        P(),
    )
    return jax.shard_map(
        functools.partial(body, mesh.shape["freq"], mesh.shape["geo"]),
        mesh=mesh,
        in_specs=placed,
        out_specs=(P("geo", "freq", None, None), P("geo", None)),
        check_vma=False,
    )
```

```python
import functools
import math

import jax
import jax.numpy as jnp
import numpy as np
from jax import lax
from jax.experimental import pallas as pl
from jax.experimental.pallas import tpu as pltpu
from jax.sharding import PartitionSpec as P

FH = 4
SUBSTEPS = 8


gravity = 9.81
base_freq = 0.03
freq_ratio = 1.05
cell_size = 20.0
sub_step = 2.0
coupling = 0.01
coef_plus = 0.4096
coef_minus = 3.1605
coef_both = 2.589


def padded(block, sides, width):
    for axis, dim in sides:
        count = lax.axis_size(axis)
        forward = [(i, i + 1) for i in range(count - 1)]
        backward = [(target, source) for source, target in forward]
        low = lax.ppermute(
            lax.slice_in_dim(block, block.shape[dim] - width, None, axis=dim), axis, forward
        )
        high = lax.ppermute(lax.slice_in_dim(block, 0, width, axis=dim), axis, backward)
        block = jnp.concatenate([low, block, high], axis=dim)
    return block


def physics(radian_freq, water_depth, dir_count):
    square = (radian_freq * radian_freq)[None, :, None]
    column = water_depth[:, None, :]
    depth_ratio = square * column / gravity
    depth_wave = depth_ratio / jnp.sqrt(jnp.tanh(depth_ratio))
    group_speed = (
        radian_freq[None, :, None]
        * column
        / depth_wave
        * (0.5 + depth_wave / jnp.sinh(2.0 * depth_wave))
    )
    orbit_weight = (
        square
        / jnp.sinh(depth_wave) ** 2
        * (radian_freq * (freq_ratio - 1.0))[None, :, None]
        * (2.0 * math.pi / dir_count)
    )
    return (group_speed, orbit_weight)


def angles_of(dir_count):
    angles = (jnp.arange(dir_count, dtype=jnp.float32) + 0.5) * (2.0 * math.pi / dir_count)
    return (jnp.cos(angles), jnp.sin(angles))


def shifted(doubled, freq_off, dir_off, count):
    dir_count = doubled.shape[2] // 2
    starts = (
        jnp.zeros((), jnp.int32),
        freq_off + FH,
        dir_off % dir_count,
        jnp.zeros((), jnp.int32),
    )
    return lax.dynamic_slice(
        doubled, starts, (doubled.shape[0], count, dir_count, doubled.shape[3])
    )


def interaction(extended, masked, quad_offsets, quad_weights):
    count = masked.shape[1]
    doubled = jnp.concatenate([extended, extended], axis=2)
    up_bins, down_bins, up_turn, down_turn = (
        quad_offsets[0],
        quad_offsets[1],
        quad_offsets[2],
        quad_offsets[3],
    )
    weight_up, weight_down = (quad_weights[0], quad_weights[1])
    upper = weight_up * shifted(doubled, up_bins, up_turn, count) + (1.0 - weight_up) * shifted(
        doubled, up_bins + 1, up_turn, count
    )
    lower = weight_down * shifted(doubled, -down_bins, -down_turn, count) + (
        1.0 - weight_down
    ) * shifted(doubled, -down_bins - 1, -down_turn, count)
    return coupling * (
        masked * masked * (coef_plus * upper + coef_minus * lower)
        - coef_both * masked * upper * lower
    )


def redistribute(extended, transfer, quad_offsets, quad_weights):
    count = transfer.shape[1]
    doubled = jnp.concatenate([extended, extended], axis=2)
    up_bins, down_bins, up_turn, down_turn = (
        quad_offsets[0],
        quad_offsets[1],
        quad_offsets[2],
        quad_offsets[3],
    )
    weight_up, weight_down = (quad_weights[0], quad_weights[1])
    gained = weight_up * shifted(doubled, -up_bins, -up_turn, count) + (1.0 - weight_up) * shifted(
        doubled, -up_bins - 1, -up_turn, count
    )
    gained = (
        gained
        + weight_down * shifted(doubled, down_bins, down_turn, count)
        + (1.0 - weight_down) * shifted(doubled, down_bins + 1, down_turn, count)
    )
    return gained - 2.0 * transfer


def east_west(east_flux, cosines):
    zeros = jnp.zeros_like(east_flux[..., :1])
    behind = jnp.concatenate([zeros, east_flux[..., :-1]], axis=-1)
    ahead = jnp.concatenate([east_flux[..., 1:], zeros], axis=-1)
    east_going = (cosines > 0.0).astype(jnp.float32)[None, None, :, None]
    return east_going * (east_flux - behind) + (1.0 - east_going) * (ahead - east_flux)


def plain_body(energy, water_depth, wet_mask, vegetation, canopy, quad_offsets, quad_weights):
    tile_rows, freq_count, dir_count, tile_cols = energy.shape
    wet_field = wet_mask.astype(jnp.float32)
    veg_field = vegetation.astype(jnp.float32)
    wet_four = wet_field[:, None, None, :]
    masked = wet_four * energy
    first_bin = lax.axis_index("freq") * freq_count
    bin_index = (first_bin + jnp.arange(freq_count, dtype=jnp.int32)).astype(jnp.float32)
    radian_freq = 2.0 * math.pi * base_freq * jnp.power(freq_ratio, bin_index)
    group_speed, orbit_weight = physics(radian_freq, water_depth, dir_count)
    partial_value = jnp.sum(orbit_weight * jnp.sum(energy, axis=2), axis=1)
    orbital = jnp.sqrt(lax.psum(partial_value, "freq"))
    full_step = SUBSTEPS * sub_step
    damping = 1.0 + full_step * canopy * veg_field * orbital
    extended = padded(masked, (("freq", 1),), FH)
    transfer = interaction(extended, masked, quad_offsets, quad_weights)
    spread = padded(transfer, (("freq", 1),), FH)
    change = redistribute(spread, transfer, quad_offsets, quad_weights)
    increment = (masked + full_step * change) / damping[:, None, None, :] - masked
    cosines, sines = angles_of(dir_count)
    step_ratio = sub_step / cell_size
    east_speed = group_speed[:, :, None, :] * cosines[None, None, :, None]
    north_speed = group_speed[:, :, None, :] * sines[None, None, :, None]
    north_going = (sines > 0.0).astype(jnp.float32)[None, None, :, None]
    spectrum = masked
    for substep in range(SUBSTEPS):
        east_flux = east_speed * spectrum
        north_flux = north_speed * spectrum
        rimmed = padded(north_flux, (("geo", 0),), 1)
        below = rimmed[:-2]
        above = rimmed[2:]
        along = north_going * (north_flux - below) + (1.0 - north_going) * (above - north_flux)
        spectrum = wet_four * (spectrum - step_ratio * (east_west(east_flux, cosines) + along))
    return (wet_four * (spectrum + increment), orbital)


MESH = pl.DeviceIdType.MESH
ROWS = 4
REACH = 8
PART = 3


def sinh_of(x):
    square = x * x
    series = 1.0 + square / 210.0
    for term in (156.0, 110.0, 72.0, 42.0, 20.0, 6.0):
        series = 1.0 + square / term * series
    wide = jnp.exp(x)
    return jnp.where(x < 1.7, x * series, 0.5 * (wide - 1.0 / wide))


def tanh_of(x):
    low = sinh_of(jnp.minimum(x, 1.0))
    fall = jnp.exp(-2.0 * x)
    return jnp.where(x < 1.0, low / jnp.sqrt(1.0 + low * low), (1.0 - fall) / (1.0 + fall))


def kernel(
    groups,
    tiles,
    dirs,
    quad_offsets,
    quad_weights,
    coefs,
    energy,
    radian,
    depth,
    wet_mask,
    vegetation,
    canopy,
    out,
    orbital,
    loaded,
    stored,
    ext,
    quads,
    spec,
    incr,
    inbox,
    outbox,
    speed,
    wet,
    drag,
    part_mine,
    part_theirs,
    send_sem,
    recv_sem,
    fringe_sems,
    part_sems,
    orbit_row,
    load_sem,
    store_sem,
    orbit_sem,
):
    bins = energy.shape[2]
    quarter = dirs // 4
    parts = quarter // PART
    mine = lax.axis_index("freq")
    tile = lax.axis_index("geo")
    has_below = tile > 0
    has_above = tile < tiles - 1
    below_id = jnp.maximum(tile - 1, 0)
    above_id = jnp.minimum(tile + 1, tiles - 1)

    def load(row, side):
        some = pl.ds(side * 2 * quarter, 2 * quarter)
        return pltpu.make_async_copy(
            energy.at[row, some], loaded.at[row, some], load_sem.at[row, side]
        )

    urgent = ((ROWS - 1, 0), (0, 1))
    later = [(row, side) for row in range(ROWS) for side in range(2) if (row, side) not in urgent]
    for row, side in (*urgent, *later):
        load(row, side).start()

    barrier = pltpu.get_barrier_semaphore()
    pl.semaphore_signal(barrier, inc=1, device_id=(1 - mine, tile), device_id_type=MESH)

    @pl.when(has_below)
    def _():
        pl.semaphore_signal(barrier, inc=1, device_id=(mine, below_id), device_id_type=MESH)

    @pl.when(has_above)
    def _():
        pl.semaphore_signal(barrier, inc=1, device_id=(mine, above_id), device_id_type=MESH)

    first = pl.multiple_of(mine * bins, 8)
    freq = radian[pl.ds(first, bins), :]
    square = freq * freq
    for row in range(ROWS):
        column = jnp.broadcast_to(depth[row : row + 1, :], (bins, 128))
        ratio = square * column / gravity
        wave = ratio / jnp.sqrt(tanh_of(ratio))
        speed[row] = (sub_step / cell_size) * (
            freq * column / wave * (0.5 + wave / sinh_of(2.0 * wave))
        )
        wet[row] = jnp.broadcast_to(wet_mask[row : row + 1, :].astype(jnp.float32), (bins, 128))

    def edge(step, q, k):
        first_dir = q * quarter + k * PART
        north = q < 2
        return pltpu.make_async_remote_copy(
            src_ref=outbox.at[step, pl.ds(first_dir, PART)],
            dst_ref=inbox.at[step, pl.ds(first_dir, PART)],
            send_sem=send_sem.at[step, q, k],
            recv_sem=recv_sem.at[step, q, k],
            device_id=(mine, above_id if north else below_id),
            device_id_type=MESH,
        )

    def sends(q):
        return has_above if q < 2 else has_below

    def receives(q):
        return has_below if q < 2 else has_above


    empty = pl.multiple_of(mine * (REACH + bins), 8)
    leaving = pl.multiple_of(REACH + (1 - mine) * (bins - REACH), 8)

    def first_edges(k, carry):
        for q in (0, 2, 1, 3):
            row = ROWS - 1 if q < 2 else 0
            for d in range(PART):
                j = q * quarter + k * PART + d
                outbox[0, j] = speed[row] * (wet[row] * loaded[row, j])

            @pl.when(sends(q))
            def _():
                edge(0, q, k).start()

        return carry

    for row, side in urgent:
        load(row, side).wait()
    waits = 1 + has_below.astype(jnp.int32) + has_above.astype(jnp.int32)
    pl.semaphore_wait(barrier, waits)
    lax.fori_loop(0, parts, first_edges, 0)
    for row, side in later:
        load(row, side).wait()

    def fill(j, totals):
        sums = []
        for row in range(ROWS):
            raw = loaded[row, j]
            wetted = wet[row] * raw
            spec[j, row] = wetted
            ext[j, row, REACH : REACH + bins, :] = wetted
            ext[j, row, pl.ds(empty, REACH), :] = jnp.zeros((REACH, 128), jnp.float32)
            sums.append(totals[row] + raw)
        return tuple(sums)

    totals = lax.fori_loop(
        0, dirs, fill, tuple(jnp.zeros((bins, 128), jnp.float32) for _ in range(ROWS))
    )

    pieces = 3 * parts
    width = dirs // pieces

    def fringe_copy(piece):
        some = pl.ds(piece * width, width)
        return pltpu.make_async_remote_copy(
            src_ref=ext.at[some, :, pl.ds(leaving, REACH), :],
            dst_ref=ext.at[some, :, pl.ds(empty, REACH), :],
            send_sem=fringe_sems.at[0, piece],
            recv_sem=fringe_sems.at[1, piece],
            device_id=(1 - mine, tile),
            device_id_type=MESH,
        )

    @pl.when(jnp.logical_not(has_below))
    def _():
        def clear(step, carry):
            inbox[step, pl.ds(0, 2 * quarter)] = jnp.zeros((2 * quarter, bins, 128), jnp.float32)
            return carry

        lax.fori_loop(0, SUBSTEPS, clear, 0)

    @pl.when(jnp.logical_not(has_above))
    def _():
        def clear(step, carry):
            inbox[step, pl.ds(2 * quarter, 2 * quarter)] = jnp.zeros(
                (2 * quarter, bins, 128), jnp.float32
            )
            return carry

        lax.fori_loop(0, SUBSTEPS, clear, 0)

    for row in range(ROWS):
        column = jnp.broadcast_to(depth[row : row + 1, :], (bins, 128))
        ratio = square * column / gravity
        wave = ratio / jnp.sqrt(tanh_of(ratio))
        steep = sinh_of(wave)
        weight = (
            square / (steep * steep) * (freq * (freq_ratio - 1.0)) * (2.0 * math.pi / dirs)
        )
        part_mine[row] = jnp.broadcast_to(
            jnp.sum(weight * totals[row], axis=0, keepdims=True), (8, 128)
        )
    part_copy = pltpu.make_async_remote_copy(
        src_ref=part_mine,
        dst_ref=part_theirs,
        send_sem=part_sems.at[0],
        recv_sem=part_sems.at[1],
        device_id=(1 - mine, tile),
        device_id_type=MESH,
    )
    part_copy.start()

    lane = lax.broadcasted_iota(jnp.int32, (bins, 128), 1)

    def move(step, q, k, last):
        east = q in (0, 3)
        north = q < 2
        inside = (lane != (0 if east else 127)).astype(jnp.float32)
        order = range(ROWS) if north else range(ROWS - 1, -1, -1)
        for d in range(PART):
            j = q * quarter + k * PART + d
            across, along = coefs[0, j], coefs[1, j]
            both = across + along
            sideways = across * inside
            before = inbox[step, j]
            for row in order:
                held = spec[j, row]
                flux = speed[row] * held
                beside = pltpu.roll(flux, 1 if east else 127, 1)
                fresh = wet[row] * (held - both * flux + sideways * beside + along * before)
                before = flux
                if last:
                    stored[row, j] = fresh + wet[row] * incr[j, row]
                else:
                    spec[j, row] = fresh
            if not last:
                outbox[step + 1, j] = speed[row] * fresh

    def store(q, k):
        some = pl.ds(q * quarter + k * PART, PART)
        return pltpu.make_async_copy(stored.at[:, some], out.at[:, some], store_sem.at[q, k])

    def substep(step, extra=None, last=False):
        for near, far in ((0, 2), (1, 3)):

            def piece(k, carry, near=near, far=far):
                for q in (near, far):

                    @pl.when(receives(q))
                    def _():
                        edge(step, q, k).wait_recv()

                    move(step, q, k, last)
                    if last:
                        store(q, k).start()
                    else:

                        @pl.when(sends(q))
                        def _():
                            edge(step + 1, q, k).start()

                if extra is not None:
                    extra((near % 2) * parts + k)
                return carry

            lax.fori_loop(0, parts, piece, 0)

    def early_step(step, carry):
        def extra(n):
            @pl.when(n < parts)
            def _():
                fringe_copy(step * parts + n).start()

        substep(step, extra)
        return carry

    lax.fori_loop(0, 3, early_step, 0)
    substep(3)

    part_copy.wait()

    def fringe_wait(piece, carry):
        fringe_copy(piece).wait()
        return carry

    lax.fori_loop(0, pieces, fringe_wait, 0)

    for row in range(ROWS):
        total = jnp.sqrt(part_mine[row] + part_theirs[row])
        orbit_row[row : row + 1, :] = total[0:1, :]
        leaves = vegetation[row : row + 1, :].astype(jnp.float32) * canopy[row : row + 1, :]
        damping = 1.0 + (SUBSTEPS * sub_step) * leaves * total[0:1, :]
        drag[row] = jnp.broadcast_to(1.0 / damping, (bins, 128))

    orbit_copy = pltpu.make_async_copy(orbit_row, orbital, orbit_sem)
    orbit_copy.start()
    up_bins, up_turn, down_turn = quad_offsets[0], quad_offsets[2], quad_offsets[3]
    weight_up, weight_down = quad_weights[0], quad_weights[1]
    rest_up, rest_down = 1.0 - weight_up, 1.0 - weight_down
    half = REACH // 2
    span = bins + REACH

    def turned(j, turn):
        j = j + turn
        j = jnp.where(j >= dirs, j - dirs, j)
        return jnp.where(j < 0, j + dirs, j)

    def couple(j, carry):
        high, low = turned(j, up_turn), turned(j, -down_turn)
        for row in range(ROWS):
            here = ext[j, row, half : half + span, :]
            upper = (
                weight_up * ext[high, row, pl.ds(half + up_bins, span), :]
                + rest_up * ext[high, row, pl.ds(half + up_bins + 1, span), :]
            )
            lower = (
                weight_down * ext[low, row, half - 3 : half - 3 + span, :]
                + rest_down * ext[low, row, half - 4 : half - 4 + span, :]
            )
            quads[j, row] = (coupling * here) * (
                here * (coef_plus * upper + coef_minus * lower) - coef_both * (upper * lower)
            )
        return carry

    def spread(j, carry):
        back, ahead = turned(j, -up_turn), turned(j, down_turn)
        for row in range(ROWS):
            change = (
                weight_up * quads[back, row, pl.ds(half - up_bins, bins), :]
                + rest_up * quads[back, row, pl.ds(half - up_bins - 1, bins), :]
                + weight_down * quads[ahead, row, half + 3 : half + 3 + bins, :]
                + rest_down * quads[ahead, row, half + 4 : half + 4 + bins, :]
                - 2.0 * quads[j, row, half : half + bins, :]
            )
            wetted = ext[j, row, REACH : REACH + bins, :]
            incr[j, row] = (wetted + (SUBSTEPS * sub_step) * change) * drag[row] - wetted
        return carry

    def couple_step(step, carry):
        share = dirs // (4 * parts)

        def extra(n):
            first_dir = ((step - 4) * 2 * parts + n) * share
            lax.fori_loop(first_dir, first_dir + share, couple, 0)

        substep(step, extra)
        return carry

    def spread_some(n):
        share = dirs // (2 * parts)
        lax.fori_loop(n * share, (n + 1) * share, spread, 0)

    lax.fori_loop(4, 6, couple_step, 0)
    substep(SUBSTEPS - 2, spread_some)
    substep(SUBSTEPS - 1, last=True)

    def drain(step, carry):
        def piece(k, inner):
            for q in range(4):

                @pl.when(sends(q))
                def _():
                    edge(step, q, k).wait_send()

            return inner

        return lax.fori_loop(0, parts, piece, carry)

    lax.fori_loop(0, SUBSTEPS, drain, 0)
    orbit_copy.wait()

    def finish(k, carry):
        for q in range(4):
            store(q, k).wait()
        return carry

    lax.fori_loop(0, parts, finish, 0)


def kernel_body(groups, tiles, energy, water_depth, wet_mask, vegetation, canopy, offsets, weights):
    rows, bins, dirs, cols = energy.shape
    angles = (np.arange(dirs, dtype=np.float32) + np.float32(0.5)) * np.float32(
        2.0 * math.pi / dirs
    )
    coefs = np.abs(np.stack([np.cos(angles), np.sin(angles)])).astype(np.float32)
    radian = 2.0 * math.pi * base_freq * freq_ratio ** np.arange(groups * bins)
    radian = np.broadcast_to(radian.astype(np.float32)[:, None], (groups * bins, cols))
    vmem = pl.BlockSpec(memory_space=pltpu.VMEM)
    hbm = pl.BlockSpec(memory_space=pltpu.HBM)
    smem = pl.BlockSpec(memory_space=pltpu.SMEM)
    f32 = jnp.float32
    parts = dirs // 4 // PART
    moved, orbital = pl.pallas_call(
        functools.partial(kernel, groups, tiles, dirs),
        out_shape=(
            jax.ShapeDtypeStruct((rows, dirs, bins, cols), f32),
            jax.ShapeDtypeStruct((rows, cols), f32),
        ),
        in_specs=[smem] * 3 + [hbm] + [vmem] * 5,
        out_specs=(hbm, hbm),
        scratch_shapes=[
            pltpu.VMEM((rows, dirs, bins, cols), f32),
            pltpu.VMEM((rows, dirs, bins, cols), f32),
            pltpu.VMEM((dirs, rows, bins + 2 * REACH, cols), f32),
            pltpu.VMEM((dirs, rows, bins + REACH, cols), f32),
            pltpu.VMEM((dirs, rows, bins, cols), f32),
            pltpu.VMEM((dirs, rows, bins, cols), f32),
            pltpu.VMEM((SUBSTEPS, dirs, bins, cols), f32),
            pltpu.VMEM((SUBSTEPS, dirs, bins, cols), f32),
            pltpu.VMEM((rows, bins, cols), f32),
            pltpu.VMEM((rows, bins, cols), f32),
            pltpu.VMEM((rows, bins, cols), f32),
            pltpu.VMEM((rows, 8, cols), f32),
            pltpu.VMEM((rows, 8, cols), f32),
            pltpu.SemaphoreType.DMA((SUBSTEPS, 4, parts)),
            pltpu.SemaphoreType.DMA((SUBSTEPS, 4, parts)),
            pltpu.SemaphoreType.DMA((2, 3 * parts)),
            pltpu.SemaphoreType.DMA((2,)),
            pltpu.VMEM((rows, cols), f32),
            pltpu.SemaphoreType.DMA((rows, 2)),
            pltpu.SemaphoreType.DMA((4, parts)),
            pltpu.SemaphoreType.DMA(()),
        ],
        compiler_params=pltpu.CompilerParams(
            collective_id=0, has_side_effects=True, vmem_limit_bytes=48 * 1024 * 1024
        ),
    )(
        offsets,
        weights,
        jnp.asarray(coefs),
        jnp.swapaxes(energy, 1, 2),
        jnp.asarray(radian),
        water_depth,
        wet_mask,
        vegetation,
        canopy,
    )
    return jnp.swapaxes(moved, 1, 2), orbital


def body(groups, tiles, energy, *rest):
    rows, bins, dirs, cols = energy.shape
    if groups == 2 and rows == ROWS and bins % 8 == 0 and dirs % (4 * PART) == 0 and cols == 128:
        return kernel_body(groups, tiles, energy, *rest)
    return plain_body(energy, *rest)


def solution(mesh):
    placed = (
        P("geo", "freq", None, None),
        P("geo", None),
        P("geo", None),
        P("geo", None),
        P("geo", None),
        P(),
        P(),
    )
    return jax.shard_map(
        functools.partial(body, mesh.shape["freq"], mesh.shape["geo"]),
        mesh=mesh,
        in_specs=placed,
        out_specs=(P("geo", "freq", None, None), P("geo", None)),
        check_vma=False,
    )
```

```python
import functools
import math

import jax
import jax.numpy as jnp
from jax import lax
from jax.experimental import pallas as pl
from jax.experimental.pallas import tpu as pltpu
from jax.sharding import PartitionSpec as P

FH = 4
SUBSTEPS = 8


gravity = 9.81
base_freq = 0.03
freq_ratio = 1.05
cell_size = 20.0
sub_step = 2.0
coupling = 0.01
coef_plus = 0.4096
coef_minus = 3.1605
coef_both = 2.589


def padded(block, sides, width):
    for axis, dim in sides:
        count = lax.axis_size(axis)
        forward = [(i, i + 1) for i in range(count - 1)]
        backward = [(target, source) for source, target in forward]
        low = lax.ppermute(
            lax.slice_in_dim(block, block.shape[dim] - width, None, axis=dim), axis, forward
        )
        high = lax.ppermute(lax.slice_in_dim(block, 0, width, axis=dim), axis, backward)
        block = jnp.concatenate([low, block, high], axis=dim)
    return block


def physics(radian_freq, water_depth, dir_count):
    square = (radian_freq * radian_freq)[None, :, None]
    column = water_depth[:, None, :]
    depth_ratio = square * column / gravity
    depth_wave = depth_ratio / jnp.sqrt(jnp.tanh(depth_ratio))
    group_speed = (
        radian_freq[None, :, None]
        * column
        / depth_wave
        * (0.5 + depth_wave / jnp.sinh(2.0 * depth_wave))
    )
    orbit_weight = (
        square
        / jnp.sinh(depth_wave) ** 2
        * (radian_freq * (freq_ratio - 1.0))[None, :, None]
        * (2.0 * math.pi / dir_count)
    )
    return (group_speed, orbit_weight)


def angles_of(dir_count):
    angles = (jnp.arange(dir_count, dtype=jnp.float32) + 0.5) * (2.0 * math.pi / dir_count)
    return (jnp.cos(angles), jnp.sin(angles))


def shifted(doubled, freq_off, dir_off, count):
    dir_count = doubled.shape[2] // 2
    starts = (
        jnp.zeros((), jnp.int32),
        freq_off + FH,
        dir_off % dir_count,
        jnp.zeros((), jnp.int32),
    )
    return lax.dynamic_slice(
        doubled, starts, (doubled.shape[0], count, dir_count, doubled.shape[3])
    )


def interaction(extended, masked, quad_offsets, quad_weights):
    count = masked.shape[1]
    doubled = jnp.concatenate([extended, extended], axis=2)
    up_bins, down_bins, up_turn, down_turn = (
        quad_offsets[0],
        quad_offsets[1],
        quad_offsets[2],
        quad_offsets[3],
    )
    weight_up, weight_down = (quad_weights[0], quad_weights[1])
    upper = weight_up * shifted(doubled, up_bins, up_turn, count) + (1.0 - weight_up) * shifted(
        doubled, up_bins + 1, up_turn, count
    )
    lower = weight_down * shifted(doubled, -down_bins, -down_turn, count) + (
        1.0 - weight_down
    ) * shifted(doubled, -down_bins - 1, -down_turn, count)
    return coupling * (
        masked * masked * (coef_plus * upper + coef_minus * lower)
        - coef_both * masked * upper * lower
    )


def redistribute(extended, transfer, quad_offsets, quad_weights):
    count = transfer.shape[1]
    doubled = jnp.concatenate([extended, extended], axis=2)
    up_bins, down_bins, up_turn, down_turn = (
        quad_offsets[0],
        quad_offsets[1],
        quad_offsets[2],
        quad_offsets[3],
    )
    weight_up, weight_down = (quad_weights[0], quad_weights[1])
    gained = weight_up * shifted(doubled, -up_bins, -up_turn, count) + (1.0 - weight_up) * shifted(
        doubled, -up_bins - 1, -up_turn, count
    )
    gained = (
        gained
        + weight_down * shifted(doubled, down_bins, down_turn, count)
        + (1.0 - weight_down) * shifted(doubled, down_bins + 1, down_turn, count)
    )
    return gained - 2.0 * transfer


def east_west(east_flux, cosines):
    zeros = jnp.zeros_like(east_flux[..., :1])
    behind = jnp.concatenate([zeros, east_flux[..., :-1]], axis=-1)
    ahead = jnp.concatenate([east_flux[..., 1:], zeros], axis=-1)
    east_going = (cosines > 0.0).astype(jnp.float32)[None, None, :, None]
    return east_going * (east_flux - behind) + (1.0 - east_going) * (ahead - east_flux)


def plain_body(energy, water_depth, wet_mask, vegetation, canopy, quad_offsets, quad_weights):
    tile_rows, freq_count, dir_count, tile_cols = energy.shape
    wet_field = wet_mask.astype(jnp.float32)
    veg_field = vegetation.astype(jnp.float32)
    wet_four = wet_field[:, None, None, :]
    masked = wet_four * energy
    first_bin = lax.axis_index("freq") * freq_count
    bin_index = (first_bin + jnp.arange(freq_count, dtype=jnp.int32)).astype(jnp.float32)
    radian_freq = 2.0 * math.pi * base_freq * jnp.power(freq_ratio, bin_index)
    group_speed, orbit_weight = physics(radian_freq, water_depth, dir_count)
    partial_value = jnp.sum(orbit_weight * jnp.sum(energy, axis=2), axis=1)
    orbital = jnp.sqrt(lax.psum(partial_value, "freq"))
    full_step = SUBSTEPS * sub_step
    damping = 1.0 + full_step * canopy * veg_field * orbital
    extended = padded(masked, (("freq", 1),), FH)
    transfer = interaction(extended, masked, quad_offsets, quad_weights)
    spread = padded(transfer, (("freq", 1),), FH)
    change = redistribute(spread, transfer, quad_offsets, quad_weights)
    increment = (masked + full_step * change) / damping[:, None, None, :] - masked
    cosines, sines = angles_of(dir_count)
    step_ratio = sub_step / cell_size
    east_speed = group_speed[:, :, None, :] * cosines[None, None, :, None]
    north_speed = group_speed[:, :, None, :] * sines[None, None, :, None]
    north_going = (sines > 0.0).astype(jnp.float32)[None, None, :, None]
    spectrum = masked
    for substep in range(SUBSTEPS):
        east_flux = east_speed * spectrum
        north_flux = north_speed * spectrum
        rimmed = padded(north_flux, (("geo", 0),), 1)
        below = rimmed[:-2]
        above = rimmed[2:]
        along = north_going * (north_flux - below) + (1.0 - north_going) * (above - north_flux)
        spectrum = wet_four * (spectrum - step_ratio * (east_west(east_flux, cosines) + along))
    return (wet_four * (spectrum + increment), orbital)


MESH = pl.DeviceIdType.MESH
ROWS = 4
REACH = 8
PART = 3


def sinh_of(x):
    square = x * x
    series = 1.0 + square / 210.0
    for term in (156.0, 110.0, 72.0, 42.0, 20.0, 6.0):
        series = 1.0 + square / term * series
    wide = jnp.exp(x)
    return jnp.where(x < 1.7, x * series, 0.5 * (wide - 1.0 / wide))


def tanh_of(x):
    low = sinh_of(jnp.minimum(x, 1.0))
    fall = jnp.exp(-2.0 * x)
    return jnp.where(x < 1.0, low / jnp.sqrt(1.0 + low * low), (1.0 - fall) / (1.0 + fall))


def kernel(
    groups,
    tiles,
    dirs,
    quad_offsets,
    quad_weights,
    energy,
    depth_in,
    wet_in,
    vegetation_in,
    canopy_in,
    out,
    orbital,
    loaded,
    stored,
    ext,
    quads,
    spec,
    incr,
    inbox,
    outbox,
    speed,
    wet,
    drag,
    part_mine,
    part_theirs,
    send_sem,
    recv_sem,
    fringe_sems,
    part_sems,
    orbit_row,
    coefs,
    depth,
    wet_mask,
    vegetation,
    canopy,
    field_sem,
    load_sem,
    store_sem,
    orbit_sem,
):
    bins = energy.shape[2]
    quarter = dirs // 4
    parts = quarter // PART
    mine = lax.axis_index("freq")
    tile = lax.axis_index("geo")
    has_below = tile > 0
    has_above = tile < tiles - 1
    below_id = jnp.maximum(tile - 1, 0)
    above_id = jnp.minimum(tile + 1, tiles - 1)

    def load(row, side):
        some = pl.ds(side * 2 * quarter, 2 * quarter)
        return pltpu.make_async_copy(
            energy.at[row, some], loaded.at[row, some], load_sem.at[row, side]
        )

    urgent = ((ROWS - 1, 0), (0, 1))
    later = [(row, side) for row in range(ROWS) for side in range(2) if (row, side) not in urgent]
    fields = [
        pltpu.make_async_copy(source, target, field_sem.at[at])
        for at, (source, target) in enumerate(
            ((depth_in, depth), (wet_in, wet_mask), (vegetation_in, vegetation), (canopy_in, canopy))
        )
    ]
    for field in fields:
        field.start()
    for row, side in (*urgent, *later):
        load(row, side).start()

    barrier = pltpu.get_barrier_semaphore()
    pl.semaphore_signal(barrier, inc=1, device_id=(1 - mine, tile), device_id_type=MESH)

    @pl.when(has_below)
    def _():
        pl.semaphore_signal(barrier, inc=1, device_id=(mine, below_id), device_id_type=MESH)

    @pl.when(has_above)
    def _():
        pl.semaphore_signal(barrier, inc=1, device_id=(mine, above_id), device_id_type=MESH)

    for j in range(dirs):
        angle = (j + 0.5) * 2.0 * math.pi / dirs
        coefs[0, j] = jnp.float32(abs(math.cos(angle)))
        coefs[1, j] = jnp.float32(abs(math.sin(angle)))
    bin_index = lax.broadcasted_iota(jnp.int32, (bins, 128), 0) + mine * bins
    freq = jnp.full((bins, 128), 2.0 * math.pi * base_freq, jnp.float32)
    for bit in range((groups * bins - 1).bit_length()):
        chosen = jnp.bitwise_and(bin_index, 1 << bit) > 0
        freq = jnp.where(chosen, freq * (freq_ratio ** (1 << bit)), freq)
    square = freq * freq
    for field in fields:
        field.wait()
    for row in range(ROWS):
        column = jnp.broadcast_to(depth[row : row + 1, :], (bins, 128))
        ratio = square * column / gravity
        wave = ratio / jnp.sqrt(tanh_of(ratio))
        speed[row] = (sub_step / cell_size) * (
            freq * column / wave * (0.5 + wave / sinh_of(2.0 * wave))
        )
        wet[row] = jnp.broadcast_to(wet_mask[row : row + 1, :].astype(jnp.float32), (bins, 128))

    def edge(step, q, k):
        first_dir = q * quarter + k * PART
        north = q < 2
        return pltpu.make_async_remote_copy(
            src_ref=outbox.at[step, pl.ds(first_dir, PART)],
            dst_ref=inbox.at[step, pl.ds(first_dir, PART)],
            send_sem=send_sem.at[step, q, k],
            recv_sem=recv_sem.at[step, q, k],
            device_id=(mine, above_id if north else below_id),
            device_id_type=MESH,
        )

    def sends(q):
        return has_above if q < 2 else has_below

    def receives(q):
        return has_below if q < 2 else has_above


    empty = pl.multiple_of(mine * (REACH + bins), 8)
    leaving = pl.multiple_of(REACH + (1 - mine) * (bins - REACH), 8)

    def first_edges(k, carry):
        for q in (0, 2, 1, 3):
            row = ROWS - 1 if q < 2 else 0
            for d in range(PART):
                j = q * quarter + k * PART + d
                outbox[0, j] = speed[row] * (wet[row] * loaded[row, j])

            @pl.when(sends(q))
            def _():
                edge(0, q, k).start()

        return carry

    for row, side in urgent:
        load(row, side).wait()
    waits = 1 + has_below.astype(jnp.int32) + has_above.astype(jnp.int32)
    pl.semaphore_wait(barrier, waits)
    lax.fori_loop(0, parts, first_edges, 0)
    for row, side in later:
        load(row, side).wait()

    def fill(j, totals):
        sums = []
        for row in range(ROWS):
            raw = loaded[row, j]
            wetted = wet[row] * raw
            spec[j, row] = wetted
            ext[j, row, REACH : REACH + bins, :] = wetted
            ext[j, row, pl.ds(empty, REACH), :] = jnp.zeros((REACH, 128), jnp.float32)
            sums.append(totals[row] + raw)
        return tuple(sums)

    totals = lax.fori_loop(
        0, dirs, fill, tuple(jnp.zeros((bins, 128), jnp.float32) for _ in range(ROWS))
    )

    pieces = 3 * parts
    width = dirs // pieces

    def fringe_copy(piece):
        some = pl.ds(piece * width, width)
        return pltpu.make_async_remote_copy(
            src_ref=ext.at[some, :, pl.ds(leaving, REACH), :],
            dst_ref=ext.at[some, :, pl.ds(empty, REACH), :],
            send_sem=fringe_sems.at[0, piece],
            recv_sem=fringe_sems.at[1, piece],
            device_id=(1 - mine, tile),
            device_id_type=MESH,
        )

    @pl.when(jnp.logical_not(has_below))
    def _():
        def clear(step, carry):
            inbox[step, pl.ds(0, 2 * quarter)] = jnp.zeros((2 * quarter, bins, 128), jnp.float32)
            return carry

        lax.fori_loop(0, SUBSTEPS, clear, 0)

    @pl.when(jnp.logical_not(has_above))
    def _():
        def clear(step, carry):
            inbox[step, pl.ds(2 * quarter, 2 * quarter)] = jnp.zeros(
                (2 * quarter, bins, 128), jnp.float32
            )
            return carry

        lax.fori_loop(0, SUBSTEPS, clear, 0)

    for row in range(ROWS):
        column = jnp.broadcast_to(depth[row : row + 1, :], (bins, 128))
        ratio = square * column / gravity
        wave = ratio / jnp.sqrt(tanh_of(ratio))
        steep = sinh_of(wave)
        weight = (
            square / (steep * steep) * (freq * (freq_ratio - 1.0)) * (2.0 * math.pi / dirs)
        )
        part_mine[row] = jnp.broadcast_to(
            jnp.sum(weight * totals[row], axis=0, keepdims=True), (8, 128)
        )
    part_copy = pltpu.make_async_remote_copy(
        src_ref=part_mine,
        dst_ref=part_theirs,
        send_sem=part_sems.at[0],
        recv_sem=part_sems.at[1],
        device_id=(1 - mine, tile),
        device_id_type=MESH,
    )
    part_copy.start()

    lane = lax.broadcasted_iota(jnp.int32, (bins, 128), 1)

    def move(step, q, k, last):
        east = q in (0, 3)
        north = q < 2
        inside = (lane != (0 if east else 127)).astype(jnp.float32)
        order = range(ROWS) if north else range(ROWS - 1, -1, -1)
        for d in range(PART):
            j = q * quarter + k * PART + d
            across, along = coefs[0, j], coefs[1, j]
            both = across + along
            sideways = across * inside
            before = inbox[step, j]
            for row in order:
                held = spec[j, row]
                flux = speed[row] * held
                beside = pltpu.roll(flux, 1 if east else 127, 1)
                fresh = wet[row] * (held - both * flux + sideways * beside + along * before)
                before = flux
                if last:
                    stored[row, j] = fresh + wet[row] * incr[j, row]
                else:
                    spec[j, row] = fresh
            if not last:
                outbox[step + 1, j] = speed[row] * fresh

    def store(q, k):
        some = pl.ds(q * quarter + k * PART, PART)
        return pltpu.make_async_copy(stored.at[:, some], out.at[:, some], store_sem.at[q, k])

    def substep(step, extra=None, last=False):
        for near, far in ((0, 2), (1, 3)):

            def piece(k, carry, near=near, far=far):
                for q in (near, far):

                    @pl.when(receives(q))
                    def _():
                        edge(step, q, k).wait_recv()

                    move(step, q, k, last)
                    if last:
                        store(q, k).start()
                    else:

                        @pl.when(sends(q))
                        def _():
                            edge(step + 1, q, k).start()

                if extra is not None:
                    extra((near % 2) * parts + k)
                return carry

            lax.fori_loop(0, parts, piece, 0)

    def early_step(step, carry):
        def extra(n):
            @pl.when(n < parts)
            def _():
                fringe_copy(step * parts + n).start()

        substep(step, extra)
        return carry

    lax.fori_loop(0, 3, early_step, 0)
    substep(3)

    part_copy.wait()

    def fringe_wait(piece, carry):
        fringe_copy(piece).wait()
        return carry

    lax.fori_loop(0, pieces, fringe_wait, 0)

    for row in range(ROWS):
        total = jnp.sqrt(part_mine[row] + part_theirs[row])
        orbit_row[row : row + 1, :] = total[0:1, :]
        leaves = vegetation[row : row + 1, :].astype(jnp.float32) * canopy[row : row + 1, :]
        damping = 1.0 + (SUBSTEPS * sub_step) * leaves * total[0:1, :]
        drag[row] = jnp.broadcast_to(1.0 / damping, (bins, 128))

    orbit_copy = pltpu.make_async_copy(orbit_row, orbital, orbit_sem)
    orbit_copy.start()
    up_bins, up_turn, down_turn = quad_offsets[0], quad_offsets[2], quad_offsets[3]
    weight_up, weight_down = quad_weights[0], quad_weights[1]
    rest_up, rest_down = 1.0 - weight_up, 1.0 - weight_down
    half = REACH // 2
    span = bins + REACH

    def turned(j, turn):
        j = j + turn
        j = jnp.where(j >= dirs, j - dirs, j)
        return jnp.where(j < 0, j + dirs, j)

    def couple(j, carry):
        high, low = turned(j, up_turn), turned(j, -down_turn)
        for row in range(ROWS):
            here = ext[j, row, half : half + span, :]
            upper = (
                weight_up * ext[high, row, pl.ds(half + up_bins, span), :]
                + rest_up * ext[high, row, pl.ds(half + up_bins + 1, span), :]
            )
            lower = (
                weight_down * ext[low, row, half - 3 : half - 3 + span, :]
                + rest_down * ext[low, row, half - 4 : half - 4 + span, :]
            )
            quads[j, row] = (coupling * here) * (
                here * (coef_plus * upper + coef_minus * lower) - coef_both * (upper * lower)
            )
        return carry

    def spread(j, carry):
        back, ahead = turned(j, -up_turn), turned(j, down_turn)
        for row in range(ROWS):
            change = (
                weight_up * quads[back, row, pl.ds(half - up_bins, bins), :]
                + rest_up * quads[back, row, pl.ds(half - up_bins - 1, bins), :]
                + weight_down * quads[ahead, row, half + 3 : half + 3 + bins, :]
                + rest_down * quads[ahead, row, half + 4 : half + 4 + bins, :]
                - 2.0 * quads[j, row, half : half + bins, :]
            )
            wetted = ext[j, row, REACH : REACH + bins, :]
            incr[j, row] = (wetted + (SUBSTEPS * sub_step) * change) * drag[row] - wetted
        return carry

    def couple_step(step, carry):
        share = dirs // (4 * parts)

        def extra(n):
            first_dir = ((step - 4) * 2 * parts + n) * share
            lax.fori_loop(first_dir, first_dir + share, couple, 0)

        substep(step, extra)
        return carry

    def spread_some(n):
        share = dirs // (2 * parts)
        lax.fori_loop(n * share, (n + 1) * share, spread, 0)

    lax.fori_loop(4, 6, couple_step, 0)
    substep(SUBSTEPS - 2, spread_some)
    substep(SUBSTEPS - 1, last=True)

    def drain(step, carry):
        def piece(k, inner):
            for q in range(4):

                @pl.when(sends(q))
                def _():
                    edge(step, q, k).wait_send()

            return inner

        return lax.fori_loop(0, parts, piece, carry)

    lax.fori_loop(0, SUBSTEPS, drain, 0)
    orbit_copy.wait()

    def finish(k, carry):
        for q in range(4):
            store(q, k).wait()
        return carry

    lax.fori_loop(0, parts, finish, 0)


def kernel_body(groups, tiles, energy, water_depth, wet_mask, vegetation, canopy, offsets, weights):
    rows, bins, dirs, cols = energy.shape
    hbm = pl.BlockSpec(memory_space=pltpu.HBM)
    smem = pl.BlockSpec(memory_space=pltpu.SMEM)
    f32 = jnp.float32
    parts = dirs // 4 // PART
    moved, orbital = pl.pallas_call(
        functools.partial(kernel, groups, tiles, dirs),
        out_shape=(
            jax.ShapeDtypeStruct((rows, dirs, bins, cols), f32),
            jax.ShapeDtypeStruct((rows, cols), f32),
        ),
        in_specs=[smem] * 2 + [hbm] * 5,
        out_specs=(hbm, hbm),
        scratch_shapes=[
            pltpu.VMEM((rows, dirs, bins, cols), f32),
            pltpu.VMEM((rows, dirs, bins, cols), f32),
            pltpu.VMEM((dirs, rows, bins + 2 * REACH, cols), f32),
            pltpu.VMEM((dirs, rows, bins + REACH, cols), f32),
            pltpu.VMEM((dirs, rows, bins, cols), f32),
            pltpu.VMEM((dirs, rows, bins, cols), f32),
            pltpu.VMEM((SUBSTEPS, dirs, bins, cols), f32),
            pltpu.VMEM((SUBSTEPS, dirs, bins, cols), f32),
            pltpu.VMEM((rows, bins, cols), f32),
            pltpu.VMEM((rows, bins, cols), f32),
            pltpu.VMEM((rows, bins, cols), f32),
            pltpu.VMEM((rows, 8, cols), f32),
            pltpu.VMEM((rows, 8, cols), f32),
            pltpu.SemaphoreType.DMA((SUBSTEPS, 4, parts)),
            pltpu.SemaphoreType.DMA((SUBSTEPS, 4, parts)),
            pltpu.SemaphoreType.DMA((2, 3 * parts)),
            pltpu.SemaphoreType.DMA((2,)),
            pltpu.VMEM((rows, cols), f32),
            pltpu.SMEM((2, dirs), f32),
            pltpu.VMEM((rows, cols), f32),
            pltpu.VMEM((rows, cols), jnp.int32),
            pltpu.VMEM((rows, cols), jnp.int32),
            pltpu.VMEM((rows, cols), f32),
            pltpu.SemaphoreType.DMA((4,)),
            pltpu.SemaphoreType.DMA((rows, 2)),
            pltpu.SemaphoreType.DMA((4, parts)),
            pltpu.SemaphoreType.DMA(()),
        ],
        compiler_params=pltpu.CompilerParams(
            collective_id=0, has_side_effects=True, vmem_limit_bytes=63 * 1024 * 1024
        ),
    )(
        offsets,
        weights,
        jnp.swapaxes(energy, 1, 2),
        water_depth,
        wet_mask,
        vegetation,
        canopy,
    )
    return jnp.swapaxes(moved, 1, 2), orbital


def body(groups, tiles, energy, *rest):
    rows, bins, dirs, cols = energy.shape
    if groups == 2 and rows == ROWS and bins % 8 == 0 and dirs % (4 * PART) == 0 and cols == 128:
        return kernel_body(groups, tiles, energy, *rest)
    return plain_body(energy, *rest)


def solution(mesh):
    placed = (
        P("geo", "freq", None, None),
        P("geo", None),
        P("geo", None),
        P("geo", None),
        P("geo", None),
        P(),
        P(),
    )
    return jax.shard_map(
        functools.partial(body, mesh.shape["freq"], mesh.shape["geo"]),
        mesh=mesh,
        in_specs=placed,
        out_specs=(P("geo", "freq", None, None), P("geo", None)),
        check_vma=False,
    )
```

```python
import functools
import math

import jax
import jax.numpy as jnp
from jax import lax
from jax.experimental import pallas as pl
from jax.experimental.pallas import tpu as pltpu
from jax.sharding import PartitionSpec as P

FH = 4
SUBSTEPS = 8


gravity = 9.81
base_freq = 0.03
freq_ratio = 1.05
cell_size = 20.0
sub_step = 2.0
coupling = 0.01
coef_plus = 0.4096
coef_minus = 3.1605
coef_both = 2.589


def padded(block, sides, width):
    for axis, dim in sides:
        count = lax.axis_size(axis)
        forward = [(i, i + 1) for i in range(count - 1)]
        backward = [(target, source) for source, target in forward]
        low = lax.ppermute(
            lax.slice_in_dim(block, block.shape[dim] - width, None, axis=dim), axis, forward
        )
        high = lax.ppermute(lax.slice_in_dim(block, 0, width, axis=dim), axis, backward)
        block = jnp.concatenate([low, block, high], axis=dim)
    return block


def physics(radian_freq, water_depth, dir_count):
    square = (radian_freq * radian_freq)[None, :, None]
    column = water_depth[:, None, :]
    depth_ratio = square * column / gravity
    depth_wave = depth_ratio / jnp.sqrt(jnp.tanh(depth_ratio))
    group_speed = (
        radian_freq[None, :, None]
        * column
        / depth_wave
        * (0.5 + depth_wave / jnp.sinh(2.0 * depth_wave))
    )
    orbit_weight = (
        square
        / jnp.sinh(depth_wave) ** 2
        * (radian_freq * (freq_ratio - 1.0))[None, :, None]
        * (2.0 * math.pi / dir_count)
    )
    return (group_speed, orbit_weight)


def angles_of(dir_count):
    angles = (jnp.arange(dir_count, dtype=jnp.float32) + 0.5) * (2.0 * math.pi / dir_count)
    return (jnp.cos(angles), jnp.sin(angles))


def shifted(doubled, freq_off, dir_off, count):
    dir_count = doubled.shape[2] // 2
    starts = (
        jnp.zeros((), jnp.int32),
        freq_off + FH,
        dir_off % dir_count,
        jnp.zeros((), jnp.int32),
    )
    return lax.dynamic_slice(
        doubled, starts, (doubled.shape[0], count, dir_count, doubled.shape[3])
    )


def interaction(extended, masked, quad_offsets, quad_weights):
    count = masked.shape[1]
    doubled = jnp.concatenate([extended, extended], axis=2)
    up_bins, down_bins, up_turn, down_turn = (
        quad_offsets[0],
        quad_offsets[1],
        quad_offsets[2],
        quad_offsets[3],
    )
    weight_up, weight_down = (quad_weights[0], quad_weights[1])
    upper = weight_up * shifted(doubled, up_bins, up_turn, count) + (1.0 - weight_up) * shifted(
        doubled, up_bins + 1, up_turn, count
    )
    lower = weight_down * shifted(doubled, -down_bins, -down_turn, count) + (
        1.0 - weight_down
    ) * shifted(doubled, -down_bins - 1, -down_turn, count)
    return coupling * (
        masked * masked * (coef_plus * upper + coef_minus * lower)
        - coef_both * masked * upper * lower
    )


def redistribute(extended, transfer, quad_offsets, quad_weights):
    count = transfer.shape[1]
    doubled = jnp.concatenate([extended, extended], axis=2)
    up_bins, down_bins, up_turn, down_turn = (
        quad_offsets[0],
        quad_offsets[1],
        quad_offsets[2],
        quad_offsets[3],
    )
    weight_up, weight_down = (quad_weights[0], quad_weights[1])
    gained = weight_up * shifted(doubled, -up_bins, -up_turn, count) + (1.0 - weight_up) * shifted(
        doubled, -up_bins - 1, -up_turn, count
    )
    gained = (
        gained
        + weight_down * shifted(doubled, down_bins, down_turn, count)
        + (1.0 - weight_down) * shifted(doubled, down_bins + 1, down_turn, count)
    )
    return gained - 2.0 * transfer


def east_west(east_flux, cosines):
    zeros = jnp.zeros_like(east_flux[..., :1])
    behind = jnp.concatenate([zeros, east_flux[..., :-1]], axis=-1)
    ahead = jnp.concatenate([east_flux[..., 1:], zeros], axis=-1)
    east_going = (cosines > 0.0).astype(jnp.float32)[None, None, :, None]
    return east_going * (east_flux - behind) + (1.0 - east_going) * (ahead - east_flux)


def plain_body(energy, water_depth, wet_mask, vegetation, canopy, quad_offsets, quad_weights):
    tile_rows, freq_count, dir_count, tile_cols = energy.shape
    wet_field = wet_mask.astype(jnp.float32)
    veg_field = vegetation.astype(jnp.float32)
    wet_four = wet_field[:, None, None, :]
    masked = wet_four * energy
    first_bin = lax.axis_index("freq") * freq_count
    bin_index = (first_bin + jnp.arange(freq_count, dtype=jnp.int32)).astype(jnp.float32)
    radian_freq = 2.0 * math.pi * base_freq * jnp.power(freq_ratio, bin_index)
    group_speed, orbit_weight = physics(radian_freq, water_depth, dir_count)
    partial_value = jnp.sum(orbit_weight * jnp.sum(energy, axis=2), axis=1)
    orbital = jnp.sqrt(lax.psum(partial_value, "freq"))
    full_step = SUBSTEPS * sub_step
    damping = 1.0 + full_step * canopy * veg_field * orbital
    extended = padded(masked, (("freq", 1),), FH)
    transfer = interaction(extended, masked, quad_offsets, quad_weights)
    spread = padded(transfer, (("freq", 1),), FH)
    change = redistribute(spread, transfer, quad_offsets, quad_weights)
    increment = (masked + full_step * change) / damping[:, None, None, :] - masked
    cosines, sines = angles_of(dir_count)
    step_ratio = sub_step / cell_size
    east_speed = group_speed[:, :, None, :] * cosines[None, None, :, None]
    north_speed = group_speed[:, :, None, :] * sines[None, None, :, None]
    north_going = (sines > 0.0).astype(jnp.float32)[None, None, :, None]
    spectrum = masked
    for substep in range(SUBSTEPS):
        east_flux = east_speed * spectrum
        north_flux = north_speed * spectrum
        rimmed = padded(north_flux, (("geo", 0),), 1)
        below = rimmed[:-2]
        above = rimmed[2:]
        along = north_going * (north_flux - below) + (1.0 - north_going) * (above - north_flux)
        spectrum = wet_four * (spectrum - step_ratio * (east_west(east_flux, cosines) + along))
    return (wet_four * (spectrum + increment), orbital)


MESH = pl.DeviceIdType.MESH
ROWS = 4
REACH = 8
PART = 3
LAG = 2


def sinh_of(x):
    square = x * x
    series = 1.0 + square / 210.0
    for term in (156.0, 110.0, 72.0, 42.0, 20.0, 6.0):
        series = 1.0 + square / term * series
    wide = jnp.exp(x)
    return jnp.where(x < 1.7, x * series, 0.5 * (wide - 1.0 / wide))


def tanh_of(x):
    low = sinh_of(jnp.minimum(x, 1.0))
    fall = jnp.exp(-2.0 * x)
    return jnp.where(x < 1.0, low / jnp.sqrt(1.0 + low * low), (1.0 - fall) / (1.0 + fall))


def kernel(
    groups,
    tiles,
    dirs,
    quad_offsets,
    quad_weights,
    energy,
    depth_in,
    wet_in,
    vegetation_in,
    canopy_in,
    out,
    orbital,
    loaded,
    stored,
    ext,
    quads,
    spec,
    incr,
    inbox,
    outbox,
    relay,
    speed,
    wet,
    drag,
    part_mine,
    part_theirs,
    send_sem,
    recv_sem,
    relay_sems,
    fringe_sems,
    part_sems,
    orbit_row,
    coefs,
    depth,
    wet_mask,
    vegetation,
    canopy,
    field_sem,
    load_sem,
    store_sem,
    orbit_sem,
):
    bins = energy.shape[2]
    quarter = dirs // 4
    parts = quarter // PART
    mine = lax.axis_index("freq")
    tile = lax.axis_index("geo")
    has_below = tile > 0
    has_above = tile < tiles - 1
    below_id = jnp.maximum(tile - 1, 0)
    above_id = jnp.minimum(tile + 1, tiles - 1)

    def load(row, side):
        some = pl.ds(side * 2 * quarter, 2 * quarter)
        return pltpu.make_async_copy(
            energy.at[row, some], loaded.at[row, some], load_sem.at[row, side]
        )

    urgent = ((ROWS - 1, 0), (0, 1))
    later = [(row, side) for row in range(ROWS) for side in range(2) if (row, side) not in urgent]
    fields = [
        pltpu.make_async_copy(source, target, field_sem.at[at])
        for at, (source, target) in enumerate(
            ((depth_in, depth), (wet_in, wet_mask), (vegetation_in, vegetation), (canopy_in, canopy))
        )
    ]
    for field in fields:
        field.start()
    for row, side in (*urgent, *later):
        load(row, side).start()

    barrier = pltpu.get_barrier_semaphore()
    pl.semaphore_signal(barrier, inc=1, device_id=(1 - mine, tile), device_id_type=MESH)

    @pl.when(has_below)
    def _():
        pl.semaphore_signal(barrier, inc=1, device_id=(mine, below_id), device_id_type=MESH)

    @pl.when(has_above)
    def _():
        pl.semaphore_signal(barrier, inc=1, device_id=(mine, above_id), device_id_type=MESH)

    planes = tiles // 4
    place = lax.rem(tile, 4)
    plane_here = lax.div(tile, 4)
    friends = ((0, has_below, 2), (1, tile < tiles - 4, 3), (2, tile > 3, -3), (3, has_above, -2))
    for at, active, offset in friends:

        @pl.when(jnp.logical_and(place == at, active))
        def _():
            pl.semaphore_signal(barrier, inc=1, device_id=(mine, tile + offset), device_id_type=MESH)

    for j in range(dirs):
        angle = (j + 0.5) * 2.0 * math.pi / dirs
        coefs[0, j] = jnp.float32(abs(math.cos(angle)))
        coefs[1, j] = jnp.float32(abs(math.sin(angle)))
    bin_index = lax.broadcasted_iota(jnp.int32, (bins, 128), 0) + mine * bins
    freq = jnp.full((bins, 128), 2.0 * math.pi * base_freq, jnp.float32)
    for bit in range((groups * bins - 1).bit_length()):
        chosen = jnp.bitwise_and(bin_index, 1 << bit) > 0
        freq = jnp.where(chosen, freq * (freq_ratio ** (1 << bit)), freq)
    square = freq * freq
    for field in fields:
        field.wait()
    for row in range(ROWS):
        column = jnp.broadcast_to(depth[row : row + 1, :], (bins, 128))
        ratio = square * column / gravity
        wave = ratio / jnp.sqrt(tanh_of(ratio))
        speed[row] = (sub_step / cell_size) * (
            freq * column / wave * (0.5 + wave / sinh_of(2.0 * wave))
        )
        wet[row] = jnp.broadcast_to(wet_mask[row : row + 1, :].astype(jnp.float32), (bins, 128))

    def edge(step, q, k):
        first_dir = q * quarter + k * PART
        north = q < 2
        return pltpu.make_async_remote_copy(
            src_ref=outbox.at[step, pl.ds(first_dir, PART)],
            dst_ref=inbox.at[step, pl.ds(first_dir, PART)],
            send_sem=send_sem.at[step, q, k],
            recv_sem=recv_sem.at[step, q, k],
            device_id=(mine, above_id if north else below_id),
            device_id_type=MESH,
        )

    def sends(q):
        return has_above if q < 2 else has_below

    def receives(q):
        return has_below if q < 2 else has_above


    empty = pl.multiple_of(mine * (REACH + bins), 8)
    leaving = pl.multiple_of(REACH + (1 - mine) * (bins - REACH), 8)

    count = 2 * parts
    crosses = {
        True: jnp.logical_and(place == 3, has_above),
        False: jnp.logical_and(place == 0, has_below),
    }
    crossing_plane = {True: plane_here, False: plane_here - 1}
    relays = {
        True: jnp.logical_and(place == 2, tile > 3),
        False: jnp.logical_and(place == 1, tile < tiles - 4),
    }
    relay_plane = {True: plane_here - 1, False: plane_here}
    to_relay = {True: 3, False: -3}
    from_relay = {True: -2, False: 2}

    def detours(plane, north, message):
        share = plane + 1 if north else planes - 1 - plane
        return lax.div((message + 1) * share, planes) > lax.div(message * share, planes)

    def first_hop(step, n, north):
        base = 0 if north else 2 * quarter
        return pltpu.make_async_remote_copy(
            src_ref=outbox.at[step, pl.ds(base + n * PART, PART)],
            dst_ref=relay.at[step, pl.ds(n * PART, PART)],
            send_sem=send_sem.at[step, (0 if north else 2) + lax.div(n, parts), lax.rem(n, parts)],
            recv_sem=relay_sems.at[1, step, n],
            device_id=(mine, tile + to_relay[north]),
            device_id_type=MESH,
        )

    def second_hop(step, n, north):
        base = 0 if north else 2 * quarter
        return pltpu.make_async_remote_copy(
            src_ref=relay.at[step, pl.ds(n * PART, PART)],
            dst_ref=inbox.at[step, pl.ds(base + n * PART, PART)],
            send_sem=relay_sems.at[0, step, n],
            recv_sem=recv_sem.at[step, (0 if north else 2) + lax.div(n, parts), lax.rem(n, parts)],
            device_id=(mine, tile + from_relay[north]),
            device_id_type=MESH,
        )

    def send(step, q, k):
        north = q < 2
        n = (q % 2) * parts + k
        around = jnp.logical_and(
            crosses[north], detours(crossing_plane[north], north, step * count + n)
        )

        @pl.when(jnp.logical_and(sends(q), jnp.logical_not(around)))
        def _():
            edge(step, q, k).start()

        @pl.when(around)
        def _():
            first_hop(step, n, north).start()

    def forward(message):
        step, n = lax.div(message, count), lax.rem(message, count)
        for north in (True, False):

            @pl.when(
                jnp.logical_and(
                    jnp.logical_and(relays[north], message < SUBSTEPS * count),
                    detours(relay_plane[north], north, message),
                )
            )
            def _():
                first_hop(step, n, north).wait_recv()
                second_hop(step, n, north).start()

    def forward_sent(message):
        step, n = lax.div(message, count), lax.rem(message, count)
        for north in (True, False):

            @pl.when(
                jnp.logical_and(relays[north], detours(relay_plane[north], north, message))
            )
            def _():
                second_hop(step, n, north).wait_send()

    def first_edges(k, carry):
        for q in (0, 2, 1, 3):
            row = ROWS - 1 if q < 2 else 0
            for d in range(PART):
                j = q * quarter + k * PART + d
                outbox[0, j] = speed[row] * (wet[row] * loaded[row, j])

            send(0, q, k)

        return carry

    for row, side in urgent:
        load(row, side).wait()
    waits = 1 + has_below.astype(jnp.int32) + has_above.astype(jnp.int32)
    for at, active, offset in friends:
        waits = waits + jnp.logical_and(place == at, active).astype(jnp.int32)
    pl.semaphore_wait(barrier, waits)
    lax.fori_loop(0, parts, first_edges, 0)
    for row, side in later:
        load(row, side).wait()

    def fill(j, totals):
        sums = []
        for row in range(ROWS):
            raw = loaded[row, j]
            wetted = wet[row] * raw
            spec[j, row] = wetted
            ext[j, row, REACH : REACH + bins, :] = wetted
            ext[j, row, pl.ds(empty, REACH), :] = jnp.zeros((REACH, 128), jnp.float32)
            sums.append(totals[row] + raw)
        return tuple(sums)

    totals = lax.fori_loop(
        0, dirs, fill, tuple(jnp.zeros((bins, 128), jnp.float32) for _ in range(ROWS))
    )

    pieces = 3 * parts
    width = dirs // pieces

    def fringe_copy(piece):
        some = pl.ds(piece * width, width)
        return pltpu.make_async_remote_copy(
            src_ref=ext.at[some, :, pl.ds(leaving, REACH), :],
            dst_ref=ext.at[some, :, pl.ds(empty, REACH), :],
            send_sem=fringe_sems.at[0, piece],
            recv_sem=fringe_sems.at[1, piece],
            device_id=(1 - mine, tile),
            device_id_type=MESH,
        )

    @pl.when(jnp.logical_not(has_below))
    def _():
        def clear(step, carry):
            inbox[step, pl.ds(0, 2 * quarter)] = jnp.zeros((2 * quarter, bins, 128), jnp.float32)
            return carry

        lax.fori_loop(0, SUBSTEPS, clear, 0)

    @pl.when(jnp.logical_not(has_above))
    def _():
        def clear(step, carry):
            inbox[step, pl.ds(2 * quarter, 2 * quarter)] = jnp.zeros(
                (2 * quarter, bins, 128), jnp.float32
            )
            return carry

        lax.fori_loop(0, SUBSTEPS, clear, 0)

    for row in range(ROWS):
        column = jnp.broadcast_to(depth[row : row + 1, :], (bins, 128))
        ratio = square * column / gravity
        wave = ratio / jnp.sqrt(tanh_of(ratio))
        steep = sinh_of(wave)
        weight = (
            square / (steep * steep) * (freq * (freq_ratio - 1.0)) * (2.0 * math.pi / dirs)
        )
        part_mine[row] = jnp.broadcast_to(
            jnp.sum(weight * totals[row], axis=0, keepdims=True), (8, 128)
        )
    part_copy = pltpu.make_async_remote_copy(
        src_ref=part_mine,
        dst_ref=part_theirs,
        send_sem=part_sems.at[0],
        recv_sem=part_sems.at[1],
        device_id=(1 - mine, tile),
        device_id_type=MESH,
    )
    part_copy.start()

    lane = lax.broadcasted_iota(jnp.int32, (bins, 128), 1)

    def move(step, q, k, last):
        east = q in (0, 3)
        north = q < 2
        inside = (lane != (0 if east else 127)).astype(jnp.float32)
        order = range(ROWS) if north else range(ROWS - 1, -1, -1)
        for d in range(PART):
            j = q * quarter + k * PART + d
            across, along = coefs[0, j], coefs[1, j]
            both = across + along
            sideways = across * inside
            before = inbox[step, j]
            for row in order:
                held = spec[j, row]
                flux = speed[row] * held
                beside = pltpu.roll(flux, 1 if east else 127, 1)
                fresh = wet[row] * (held - both * flux + sideways * beside + along * before)
                before = flux
                if last:
                    stored[row, j] = fresh + wet[row] * incr[j, row]
                else:
                    spec[j, row] = fresh
            if not last:
                outbox[step + 1, j] = speed[row] * fresh

    def store(q, k):
        some = pl.ds(q * quarter + k * PART, PART)
        return pltpu.make_async_copy(stored.at[:, some], out.at[:, some], store_sem.at[q, k])

    def substep(step, extra=None, last=False):
        for near, far in ((0, 2), (1, 3)):

            def piece(k, carry, near=near, far=far):
                for q in (near, far):

                    @pl.when(receives(q))
                    def _():
                        edge(step, q, k).wait_recv()

                    move(step, q, k, last)
                    if last:
                        store(q, k).start()
                    else:
                        send(step + 1, q, k)

                forward(step * count + (near % 2) * parts + k + count - LAG)
                if extra is not None:
                    extra((near % 2) * parts + k)
                return carry

            lax.fori_loop(0, parts, piece, 0)

    def early_step(step, carry):
        def extra(n):
            @pl.when(n < parts)
            def _():
                fringe_copy(step * parts + n).start()

        substep(step, extra)
        return carry

    def forward_first(message, carry):
        forward(message)
        return carry

    lax.fori_loop(0, count - LAG, forward_first, 0)
    lax.fori_loop(0, 3, early_step, 0)
    substep(3)

    part_copy.wait()

    def fringe_wait(piece, carry):
        fringe_copy(piece).wait()
        return carry

    lax.fori_loop(0, pieces, fringe_wait, 0)

    for row in range(ROWS):
        total = jnp.sqrt(part_mine[row] + part_theirs[row])
        orbit_row[row : row + 1, :] = total[0:1, :]
        leaves = vegetation[row : row + 1, :].astype(jnp.float32) * canopy[row : row + 1, :]
        damping = 1.0 + (SUBSTEPS * sub_step) * leaves * total[0:1, :]
        drag[row] = jnp.broadcast_to(1.0 / damping, (bins, 128))

    orbit_copy = pltpu.make_async_copy(orbit_row, orbital, orbit_sem)
    orbit_copy.start()
    up_bins, up_turn, down_turn = quad_offsets[0], quad_offsets[2], quad_offsets[3]
    weight_up, weight_down = quad_weights[0], quad_weights[1]
    rest_up, rest_down = 1.0 - weight_up, 1.0 - weight_down
    half = REACH // 2
    span = bins + REACH

    def turned(j, turn):
        j = j + turn
        j = jnp.where(j >= dirs, j - dirs, j)
        return jnp.where(j < 0, j + dirs, j)

    def couple(j, carry):
        high, low = turned(j, up_turn), turned(j, -down_turn)
        for row in range(ROWS):
            here = ext[j, row, half : half + span, :]
            upper = (
                weight_up * ext[high, row, pl.ds(half + up_bins, span), :]
                + rest_up * ext[high, row, pl.ds(half + up_bins + 1, span), :]
            )
            lower = (
                weight_down * ext[low, row, half - 3 : half - 3 + span, :]
                + rest_down * ext[low, row, half - 4 : half - 4 + span, :]
            )
            quads[j, row] = (coupling * here) * (
                here * (coef_plus * upper + coef_minus * lower) - coef_both * (upper * lower)
            )
        return carry

    def spread(j, carry):
        back, ahead = turned(j, -up_turn), turned(j, down_turn)
        for row in range(ROWS):
            change = (
                weight_up * quads[back, row, pl.ds(half - up_bins, bins), :]
                + rest_up * quads[back, row, pl.ds(half - up_bins - 1, bins), :]
                + weight_down * quads[ahead, row, half + 3 : half + 3 + bins, :]
                + rest_down * quads[ahead, row, half + 4 : half + 4 + bins, :]
                - 2.0 * quads[j, row, half : half + bins, :]
            )
            wetted = ext[j, row, REACH : REACH + bins, :]
            incr[j, row] = (wetted + (SUBSTEPS * sub_step) * change) * drag[row] - wetted
        return carry

    def couple_step(step, carry):
        share = dirs // (4 * parts)

        def extra(n):
            first_dir = ((step - 4) * 2 * parts + n) * share
            lax.fori_loop(first_dir, first_dir + share, couple, 0)

        substep(step, extra)
        return carry

    def spread_some(n):
        share = dirs // (2 * parts)
        lax.fori_loop(n * share, (n + 1) * share, spread, 0)

    lax.fori_loop(4, 6, couple_step, 0)
    substep(SUBSTEPS - 2, spread_some)
    substep(SUBSTEPS - 1, last=True)

    def drain(step, carry):
        def piece(k, inner):
            for q in range(4):

                @pl.when(sends(q))
                def _():
                    edge(step, q, k).wait_send()

            return inner

        return lax.fori_loop(0, parts, piece, carry)

    lax.fori_loop(0, SUBSTEPS, drain, 0)

    def drain_relay(message, carry):
        forward_sent(message)
        return carry

    lax.fori_loop(0, SUBSTEPS * count, drain_relay, 0)
    orbit_copy.wait()

    def finish(k, carry):
        for q in range(4):
            store(q, k).wait()
        return carry

    lax.fori_loop(0, parts, finish, 0)


def hand_over(moved_in, orbital_in, moved, orbital, sems):
    half = moved.shape[1] // 2
    copies = [pltpu.make_async_copy(orbital_in, orbital, sems.at[2 * ROWS])]
    for row in range(ROWS):
        for side in range(2):
            some = pl.ds(side * half, half)
            copies.append(
                pltpu.make_async_copy(
                    moved_in.at[row, some], moved.at[row, some], sems.at[2 * row + side]
                )
            )
    for copy in copies:
        copy.start()
    for copy in copies:
        copy.wait()


def kernel_body(groups, tiles, energy, water_depth, wet_mask, vegetation, canopy, offsets, weights):
    rows, bins, dirs, cols = energy.shape
    hbm = pl.BlockSpec(memory_space=pltpu.HBM)
    anywhere = pl.BlockSpec(memory_space=pl.ANY)
    smem = pl.BlockSpec(memory_space=pltpu.SMEM)
    f32 = jnp.float32
    parts = dirs // 4 // PART
    moved, orbital = pl.pallas_call(
        functools.partial(kernel, groups, tiles, dirs),
        out_shape=(
            jax.ShapeDtypeStruct((rows, dirs, bins, cols), f32),
            jax.ShapeDtypeStruct((rows, cols), f32),
        ),
        in_specs=[smem] * 2 + [hbm] * 5,
        out_specs=(hbm, hbm),
        scratch_shapes=[
            pltpu.VMEM((rows, dirs, bins, cols), f32),
            pltpu.VMEM((rows, dirs, bins, cols), f32),
            pltpu.VMEM((dirs, rows, bins + 2 * REACH, cols), f32),
            pltpu.VMEM((dirs, rows, bins + REACH, cols), f32),
            pltpu.VMEM((dirs, rows, bins, cols), f32),
            pltpu.VMEM((dirs, rows, bins, cols), f32),
            pltpu.VMEM((SUBSTEPS, dirs, bins, cols), f32),
            pltpu.VMEM((SUBSTEPS, dirs, bins, cols), f32),
            pltpu.VMEM((SUBSTEPS, dirs // 2, bins, cols), f32),
            pltpu.VMEM((rows, bins, cols), f32),
            pltpu.VMEM((rows, bins, cols), f32),
            pltpu.VMEM((rows, bins, cols), f32),
            pltpu.VMEM((rows, 8, cols), f32),
            pltpu.VMEM((rows, 8, cols), f32),
            pltpu.SemaphoreType.DMA((SUBSTEPS, 4, parts)),
            pltpu.SemaphoreType.DMA((SUBSTEPS, 4, parts)),
            pltpu.SemaphoreType.DMA((2, SUBSTEPS, 2 * parts)),
            pltpu.SemaphoreType.DMA((2, 3 * parts)),
            pltpu.SemaphoreType.DMA((2,)),
            pltpu.VMEM((rows, cols), f32),
            pltpu.SMEM((2, dirs), f32),
            pltpu.VMEM((rows, cols), f32),
            pltpu.VMEM((rows, cols), jnp.int32),
            pltpu.VMEM((rows, cols), jnp.int32),
            pltpu.VMEM((rows, cols), f32),
            pltpu.SemaphoreType.DMA((4,)),
            pltpu.SemaphoreType.DMA((rows, 2)),
            pltpu.SemaphoreType.DMA((4, parts)),
            pltpu.SemaphoreType.DMA(()),
        ],
        compiler_params=pltpu.CompilerParams(
            collective_id=0, has_side_effects=True, vmem_limit_bytes=63 * 1024 * 1024
        ),
    )(
        offsets,
        weights,
        jnp.swapaxes(energy, 1, 2),
        water_depth,
        wet_mask,
        vegetation,
        canopy,
    )
    moved, orbital = pl.pallas_call(
        hand_over,
        out_shape=(
            jax.ShapeDtypeStruct(moved.shape, f32),
            jax.ShapeDtypeStruct(orbital.shape, f32),
        ),
        in_specs=[anywhere] * 2,
        out_specs=(anywhere, anywhere),
        scratch_shapes=[pltpu.SemaphoreType.DMA((2 * rows + 1,))],
        compiler_params=pltpu.CompilerParams(vmem_limit_bytes=63 * 1024 * 1024),
    )(moved, orbital)
    return jnp.swapaxes(moved, 1, 2), orbital


def body(groups, tiles, energy, *rest):
    rows, bins, dirs, cols = energy.shape
    if groups == 2 and rows == ROWS and bins % 8 == 0 and dirs % (4 * PART) == 0 and cols == 128 and tiles % 4 == 0:
        return kernel_body(groups, tiles, energy, *rest)
    return plain_body(energy, *rest)


def solution(mesh):
    placed = (
        P("geo", "freq", None, None),
        P("geo", None),
        P("geo", None),
        P("geo", None),
        P("geo", None),
        P(),
        P(),
    )
    return jax.shard_map(
        functools.partial(body, mesh.shape["freq"], mesh.shape["geo"]),
        mesh=mesh,
        in_specs=placed,
        out_specs=(P("geo", "freq", None, None), P("geo", None)),
        check_vma=False,
    )
```

```python
import functools
import math

import jax
import jax.numpy as jnp
from jax import lax
from jax.experimental import pallas as pl
from jax.experimental.pallas import tpu as pltpu
from jax.sharding import PartitionSpec as P

FH = 4
SUBSTEPS = 8


gravity = 9.81
base_freq = 0.03
freq_ratio = 1.05
cell_size = 20.0
sub_step = 2.0
coupling = 0.01
coef_plus = 0.4096
coef_minus = 3.1605
coef_both = 2.589


def padded(block, sides, width):
    for axis, dim in sides:
        count = lax.axis_size(axis)
        forward = [(i, i + 1) for i in range(count - 1)]
        backward = [(target, source) for source, target in forward]
        low = lax.ppermute(
            lax.slice_in_dim(block, block.shape[dim] - width, None, axis=dim), axis, forward
        )
        high = lax.ppermute(lax.slice_in_dim(block, 0, width, axis=dim), axis, backward)
        block = jnp.concatenate([low, block, high], axis=dim)
    return block


def physics(radian_freq, water_depth, dir_count):
    square = (radian_freq * radian_freq)[None, :, None]
    column = water_depth[:, None, :]
    depth_ratio = square * column / gravity
    depth_wave = depth_ratio / jnp.sqrt(jnp.tanh(depth_ratio))
    group_speed = (
        radian_freq[None, :, None]
        * column
        / depth_wave
        * (0.5 + depth_wave / jnp.sinh(2.0 * depth_wave))
    )
    orbit_weight = (
        square
        / jnp.sinh(depth_wave) ** 2
        * (radian_freq * (freq_ratio - 1.0))[None, :, None]
        * (2.0 * math.pi / dir_count)
    )
    return (group_speed, orbit_weight)


def angles_of(dir_count):
    angles = (jnp.arange(dir_count, dtype=jnp.float32) + 0.5) * (2.0 * math.pi / dir_count)
    return (jnp.cos(angles), jnp.sin(angles))


def shifted(doubled, freq_off, dir_off, count):
    dir_count = doubled.shape[2] // 2
    starts = (
        jnp.zeros((), jnp.int32),
        freq_off + FH,
        dir_off % dir_count,
        jnp.zeros((), jnp.int32),
    )
    return lax.dynamic_slice(
        doubled, starts, (doubled.shape[0], count, dir_count, doubled.shape[3])
    )


def interaction(extended, masked, quad_offsets, quad_weights):
    count = masked.shape[1]
    doubled = jnp.concatenate([extended, extended], axis=2)
    up_bins, down_bins, up_turn, down_turn = (
        quad_offsets[0],
        quad_offsets[1],
        quad_offsets[2],
        quad_offsets[3],
    )
    weight_up, weight_down = (quad_weights[0], quad_weights[1])
    upper = weight_up * shifted(doubled, up_bins, up_turn, count) + (1.0 - weight_up) * shifted(
        doubled, up_bins + 1, up_turn, count
    )
    lower = weight_down * shifted(doubled, -down_bins, -down_turn, count) + (
        1.0 - weight_down
    ) * shifted(doubled, -down_bins - 1, -down_turn, count)
    return coupling * (
        masked * masked * (coef_plus * upper + coef_minus * lower)
        - coef_both * masked * upper * lower
    )


def redistribute(extended, transfer, quad_offsets, quad_weights):
    count = transfer.shape[1]
    doubled = jnp.concatenate([extended, extended], axis=2)
    up_bins, down_bins, up_turn, down_turn = (
        quad_offsets[0],
        quad_offsets[1],
        quad_offsets[2],
        quad_offsets[3],
    )
    weight_up, weight_down = (quad_weights[0], quad_weights[1])
    gained = weight_up * shifted(doubled, -up_bins, -up_turn, count) + (1.0 - weight_up) * shifted(
        doubled, -up_bins - 1, -up_turn, count
    )
    gained = (
        gained
        + weight_down * shifted(doubled, down_bins, down_turn, count)
        + (1.0 - weight_down) * shifted(doubled, down_bins + 1, down_turn, count)
    )
    return gained - 2.0 * transfer


def east_west(east_flux, cosines):
    zeros = jnp.zeros_like(east_flux[..., :1])
    behind = jnp.concatenate([zeros, east_flux[..., :-1]], axis=-1)
    ahead = jnp.concatenate([east_flux[..., 1:], zeros], axis=-1)
    east_going = (cosines > 0.0).astype(jnp.float32)[None, None, :, None]
    return east_going * (east_flux - behind) + (1.0 - east_going) * (ahead - east_flux)


def plain_body(energy, water_depth, wet_mask, vegetation, canopy, quad_offsets, quad_weights):
    tile_rows, freq_count, dir_count, tile_cols = energy.shape
    wet_field = wet_mask.astype(jnp.float32)
    veg_field = vegetation.astype(jnp.float32)
    wet_four = wet_field[:, None, None, :]
    masked = wet_four * energy
    first_bin = lax.axis_index("freq") * freq_count
    bin_index = (first_bin + jnp.arange(freq_count, dtype=jnp.int32)).astype(jnp.float32)
    radian_freq = 2.0 * math.pi * base_freq * jnp.power(freq_ratio, bin_index)
    group_speed, orbit_weight = physics(radian_freq, water_depth, dir_count)
    partial_value = jnp.sum(orbit_weight * jnp.sum(energy, axis=2), axis=1)
    orbital = jnp.sqrt(lax.psum(partial_value, "freq"))
    full_step = SUBSTEPS * sub_step
    damping = 1.0 + full_step * canopy * veg_field * orbital
    extended = padded(masked, (("freq", 1),), FH)
    transfer = interaction(extended, masked, quad_offsets, quad_weights)
    spread = padded(transfer, (("freq", 1),), FH)
    change = redistribute(spread, transfer, quad_offsets, quad_weights)
    increment = (masked + full_step * change) / damping[:, None, None, :] - masked
    cosines, sines = angles_of(dir_count)
    step_ratio = sub_step / cell_size
    east_speed = group_speed[:, :, None, :] * cosines[None, None, :, None]
    north_speed = group_speed[:, :, None, :] * sines[None, None, :, None]
    north_going = (sines > 0.0).astype(jnp.float32)[None, None, :, None]
    spectrum = masked
    for substep in range(SUBSTEPS):
        east_flux = east_speed * spectrum
        north_flux = north_speed * spectrum
        rimmed = padded(north_flux, (("geo", 0),), 1)
        below = rimmed[:-2]
        above = rimmed[2:]
        along = north_going * (north_flux - below) + (1.0 - north_going) * (above - north_flux)
        spectrum = wet_four * (spectrum - step_ratio * (east_west(east_flux, cosines) + along))
    return (wet_four * (spectrum + increment), orbital)


MESH = pl.DeviceIdType.MESH
ROWS = 4
REACH = 8
PART = 9


def sinh_of(x):
    square = x * x
    series = 1.0 + square / 210.0
    for term in (156.0, 110.0, 72.0, 42.0, 20.0, 6.0):
        series = 1.0 + square / term * series
    wide = jnp.exp(x)
    return jnp.where(x < 1.7, x * series, 0.5 * (wide - 1.0 / wide))


def tanh_of(x):
    low = sinh_of(jnp.minimum(x, 1.0))
    fall = jnp.exp(-2.0 * x)
    return jnp.where(x < 1.0, low / jnp.sqrt(1.0 + low * low), (1.0 - fall) / (1.0 + fall))


def kernel(
    groups,
    tiles,
    dirs,
    quad_offsets,
    quad_weights,
    energy,
    depth_in,
    wet_in,
    vegetation_in,
    canopy_in,
    out,
    orbital,
    loaded,
    stored,
    ext,
    quads,
    spec,
    incr,
    inbox,
    outbox,
    speed,
    wet,
    drag,
    part_mine,
    part_theirs,
    send_sem,
    recv_sem,
    fringe_sems,
    part_sems,
    orbit_row,
    coefs,
    depth,
    wet_mask,
    vegetation,
    canopy,
    field_sem,
    load_sem,
    store_sem,
    orbit_sem,
):
    bins = energy.shape[2]
    quarter = dirs // 4
    parts = quarter // PART
    mine = lax.axis_index("freq")
    tile = lax.axis_index("geo")
    has_below = tile > 0
    has_above = tile < tiles - 1
    below_id = jnp.maximum(tile - 1, 0)
    above_id = jnp.minimum(tile + 1, tiles - 1)

    def load(row, side):
        some = pl.ds(side * 2 * quarter, 2 * quarter)
        return pltpu.make_async_copy(
            energy.at[row, some], loaded.at[row, some], load_sem.at[row, side]
        )

    urgent = ((ROWS - 1, 0), (0, 1))
    later = [(row, side) for row in range(ROWS) for side in range(2) if (row, side) not in urgent]
    fields = [
        pltpu.make_async_copy(source, target, field_sem.at[at])
        for at, (source, target) in enumerate(
            ((depth_in, depth), (wet_in, wet_mask), (vegetation_in, vegetation), (canopy_in, canopy))
        )
    ]
    for field in fields:
        field.start()
    for row, side in (*urgent, *later):
        load(row, side).start()

    barrier = pltpu.get_barrier_semaphore()
    pl.semaphore_signal(barrier, inc=1, device_id=(1 - mine, tile), device_id_type=MESH)

    @pl.when(has_below)
    def _():
        pl.semaphore_signal(barrier, inc=1, device_id=(mine, below_id), device_id_type=MESH)

    @pl.when(has_above)
    def _():
        pl.semaphore_signal(barrier, inc=1, device_id=(mine, above_id), device_id_type=MESH)

    for j in range(dirs):
        angle = (j + 0.5) * 2.0 * math.pi / dirs
        coefs[0, j] = jnp.float32(abs(math.cos(angle)))
        coefs[1, j] = jnp.float32(abs(math.sin(angle)))
    bin_index = lax.broadcasted_iota(jnp.int32, (bins, 128), 0) + mine * bins
    freq = jnp.full((bins, 128), 2.0 * math.pi * base_freq, jnp.float32)
    for bit in range((groups * bins - 1).bit_length()):
        chosen = jnp.bitwise_and(bin_index, 1 << bit) > 0
        freq = jnp.where(chosen, freq * (freq_ratio ** (1 << bit)), freq)
    square = freq * freq
    for field in fields:
        field.wait()
    for row in range(ROWS):
        column = jnp.broadcast_to(depth[row : row + 1, :], (bins, 128))
        ratio = square * column / gravity
        wave = ratio / jnp.sqrt(tanh_of(ratio))
        speed[row] = (sub_step / cell_size) * (
            freq * column / wave * (0.5 + wave / sinh_of(2.0 * wave))
        )
        wet[row] = jnp.broadcast_to(wet_mask[row : row + 1, :].astype(jnp.float32), (bins, 128))

    def edge(step, q, k):
        first_dir = q * quarter + k * PART
        north = q < 2
        return pltpu.make_async_remote_copy(
            src_ref=outbox.at[step, pl.ds(first_dir, PART)],
            dst_ref=inbox.at[step, pl.ds(first_dir, PART)],
            send_sem=send_sem.at[step, q, k],
            recv_sem=recv_sem.at[step, q, k],
            device_id=(mine, above_id if north else below_id),
            device_id_type=MESH,
        )

    def sends(q):
        return has_above if q < 2 else has_below

    def receives(q):
        return has_below if q < 2 else has_above


    empty = pl.multiple_of(mine * (REACH + bins), 8)
    leaving = pl.multiple_of(REACH + (1 - mine) * (bins - REACH), 8)

    def first_edges(k, carry):
        for q in (0, 2, 1, 3):
            row = ROWS - 1 if q < 2 else 0
            for d in range(PART):
                j = q * quarter + k * PART + d
                outbox[0, j] = speed[row] * (wet[row] * loaded[row, j])

            @pl.when(sends(q))
            def _():
                edge(0, q, k).start()

        return carry

    for row, side in urgent:
        load(row, side).wait()
    waits = 1 + has_below.astype(jnp.int32) + has_above.astype(jnp.int32)
    pl.semaphore_wait(barrier, waits)
    lax.fori_loop(0, parts, first_edges, 0)
    for row, side in later:
        load(row, side).wait()

    def fill(j, totals):
        sums = []
        for row in range(ROWS):
            raw = loaded[row, j]
            wetted = wet[row] * raw
            spec[j, row] = wetted
            ext[j, row, REACH : REACH + bins, :] = wetted
            ext[j, row, pl.ds(empty, REACH), :] = jnp.zeros((REACH, 128), jnp.float32)
            sums.append(totals[row] + raw)
        return tuple(sums)

    totals = lax.fori_loop(
        0, dirs, fill, tuple(jnp.zeros((bins, 128), jnp.float32) for _ in range(ROWS))
    )

    pieces = 3 * parts
    width = dirs // pieces

    def fringe_copy(piece):
        some = pl.ds(piece * width, width)
        return pltpu.make_async_remote_copy(
            src_ref=ext.at[some, :, pl.ds(leaving, REACH), :],
            dst_ref=ext.at[some, :, pl.ds(empty, REACH), :],
            send_sem=fringe_sems.at[0, piece],
            recv_sem=fringe_sems.at[1, piece],
            device_id=(1 - mine, tile),
            device_id_type=MESH,
        )

    @pl.when(jnp.logical_not(has_below))
    def _():
        def clear(step, carry):
            inbox[step, pl.ds(0, 2 * quarter)] = jnp.zeros((2 * quarter, bins, 128), jnp.float32)
            return carry

        lax.fori_loop(0, SUBSTEPS, clear, 0)

    @pl.when(jnp.logical_not(has_above))
    def _():
        def clear(step, carry):
            inbox[step, pl.ds(2 * quarter, 2 * quarter)] = jnp.zeros(
                (2 * quarter, bins, 128), jnp.float32
            )
            return carry

        lax.fori_loop(0, SUBSTEPS, clear, 0)

    for row in range(ROWS):
        column = jnp.broadcast_to(depth[row : row + 1, :], (bins, 128))
        ratio = square * column / gravity
        wave = ratio / jnp.sqrt(tanh_of(ratio))
        steep = sinh_of(wave)
        weight = (
            square / (steep * steep) * (freq * (freq_ratio - 1.0)) * (2.0 * math.pi / dirs)
        )
        part_mine[row] = jnp.broadcast_to(
            jnp.sum(weight * totals[row], axis=0, keepdims=True), (8, 128)
        )
    part_copy = pltpu.make_async_remote_copy(
        src_ref=part_mine,
        dst_ref=part_theirs,
        send_sem=part_sems.at[0],
        recv_sem=part_sems.at[1],
        device_id=(1 - mine, tile),
        device_id_type=MESH,
    )
    part_copy.start()

    lane = lax.broadcasted_iota(jnp.int32, (bins, 128), 1)

    def move(step, q, k, last):
        east = q in (0, 3)
        north = q < 2
        inside = (lane != (0 if east else 127)).astype(jnp.float32)
        order = range(ROWS) if north else range(ROWS - 1, -1, -1)
        for d in range(PART):
            j = q * quarter + k * PART + d
            across, along = coefs[0, j], coefs[1, j]
            both = across + along
            sideways = across * inside
            before = inbox[step, j]
            for row in order:
                held = spec[j, row]
                flux = speed[row] * held
                beside = pltpu.roll(flux, 1 if east else 127, 1)
                fresh = wet[row] * (held - both * flux + sideways * beside + along * before)
                before = flux
                if last:
                    stored[row, j] = fresh + wet[row] * incr[j, row]
                else:
                    spec[j, row] = fresh
            if not last:
                outbox[step + 1, j] = speed[row] * fresh

    def store(q, k):
        some = pl.ds(q * quarter + k * PART, PART)
        return pltpu.make_async_copy(stored.at[:, some], out.at[:, some], store_sem.at[q, k])

    def substep(step, extra=None, last=False):
        for near, far in ((0, 2), (1, 3)):

            def piece(k, carry, near=near, far=far):
                for q in (near, far):

                    @pl.when(receives(q))
                    def _():
                        edge(step, q, k).wait_recv()

                    move(step, q, k, last)
                    if last:
                        store(q, k).start()
                    else:

                        @pl.when(sends(q))
                        def _():
                            edge(step + 1, q, k).start()

                if extra is not None:
                    extra((near % 2) * parts + k)
                return carry

            lax.fori_loop(0, parts, piece, 0)

    def early_step(step, carry):
        def extra(n):
            @pl.when(n < parts)
            def _():
                fringe_copy(step * parts + n).start()

        substep(step, extra)
        return carry

    lax.fori_loop(0, 3, early_step, 0)
    substep(3)

    part_copy.wait()

    def fringe_wait(piece, carry):
        fringe_copy(piece).wait()
        return carry

    lax.fori_loop(0, pieces, fringe_wait, 0)

    for row in range(ROWS):
        total = jnp.sqrt(part_mine[row] + part_theirs[row])
        orbit_row[row : row + 1, :] = total[0:1, :]
        leaves = vegetation[row : row + 1, :].astype(jnp.float32) * canopy[row : row + 1, :]
        damping = 1.0 + (SUBSTEPS * sub_step) * leaves * total[0:1, :]
        drag[row] = jnp.broadcast_to(1.0 / damping, (bins, 128))

    orbit_copy = pltpu.make_async_copy(orbit_row, orbital, orbit_sem)
    orbit_copy.start()
    up_bins, up_turn, down_turn = quad_offsets[0], quad_offsets[2], quad_offsets[3]
    weight_up, weight_down = quad_weights[0], quad_weights[1]
    rest_up, rest_down = 1.0 - weight_up, 1.0 - weight_down
    half = REACH // 2
    span = bins + REACH

    def turned(j, turn):
        j = j + turn
        j = jnp.where(j >= dirs, j - dirs, j)
        return jnp.where(j < 0, j + dirs, j)

    def couple(j, carry):
        high, low = turned(j, up_turn), turned(j, -down_turn)
        for row in range(ROWS):
            here = ext[j, row, half : half + span, :]
            upper = (
                weight_up * ext[high, row, pl.ds(half + up_bins, span), :]
                + rest_up * ext[high, row, pl.ds(half + up_bins + 1, span), :]
            )
            lower = (
                weight_down * ext[low, row, half - 3 : half - 3 + span, :]
                + rest_down * ext[low, row, half - 4 : half - 4 + span, :]
            )
            quads[j, row] = (coupling * here) * (
                here * (coef_plus * upper + coef_minus * lower) - coef_both * (upper * lower)
            )
        return carry

    def spread(j, carry):
        back, ahead = turned(j, -up_turn), turned(j, down_turn)
        for row in range(ROWS):
            change = (
                weight_up * quads[back, row, pl.ds(half - up_bins, bins), :]
                + rest_up * quads[back, row, pl.ds(half - up_bins - 1, bins), :]
                + weight_down * quads[ahead, row, half + 3 : half + 3 + bins, :]
                + rest_down * quads[ahead, row, half + 4 : half + 4 + bins, :]
                - 2.0 * quads[j, row, half : half + bins, :]
            )
            wetted = ext[j, row, REACH : REACH + bins, :]
            incr[j, row] = (wetted + (SUBSTEPS * sub_step) * change) * drag[row] - wetted
        return carry

    def couple_step(step, carry):
        share = dirs // (4 * parts)

        def extra(n):
            first_dir = ((step - 4) * 2 * parts + n) * share
            lax.fori_loop(first_dir, first_dir + share, couple, 0)

        substep(step, extra)
        return carry

    def spread_some(n):
        share = dirs // (2 * parts)
        lax.fori_loop(n * share, (n + 1) * share, spread, 0)

    lax.fori_loop(4, 6, couple_step, 0)
    substep(SUBSTEPS - 2, spread_some)
    substep(SUBSTEPS - 1, last=True)

    def drain(step, carry):
        def piece(k, inner):
            for q in range(4):

                @pl.when(sends(q))
                def _():
                    edge(step, q, k).wait_send()

            return inner

        return lax.fori_loop(0, parts, piece, carry)

    lax.fori_loop(0, SUBSTEPS, drain, 0)
    orbit_copy.wait()

    def finish(k, carry):
        for q in range(4):
            store(q, k).wait()
        return carry

    lax.fori_loop(0, parts, finish, 0)


def hand_over(moved_in, orbital_in, moved, orbital):
    moved[...] = moved_in[...]
    orbital[...] = orbital_in[...]


def kernel_body(groups, tiles, energy, water_depth, wet_mask, vegetation, canopy, offsets, weights):
    rows, bins, dirs, cols = energy.shape
    hbm = pl.BlockSpec(memory_space=pltpu.HBM)
    smem = pl.BlockSpec(memory_space=pltpu.SMEM)
    f32 = jnp.float32
    parts = dirs // 4 // PART
    moved, orbital = pl.pallas_call(
        functools.partial(kernel, groups, tiles, dirs),
        out_shape=(
            jax.ShapeDtypeStruct((rows, dirs, bins, cols), f32),
            jax.ShapeDtypeStruct((rows, cols), f32),
        ),
        in_specs=[smem] * 2 + [hbm] * 5,
        out_specs=(hbm, hbm),
        scratch_shapes=[
            pltpu.VMEM((rows, dirs, bins, cols), f32),
            pltpu.VMEM((rows, dirs, bins, cols), f32),
            pltpu.VMEM((dirs, rows, bins + 2 * REACH, cols), f32),
            pltpu.VMEM((dirs, rows, bins + REACH, cols), f32),
            pltpu.VMEM((dirs, rows, bins, cols), f32),
            pltpu.VMEM((dirs, rows, bins, cols), f32),
            pltpu.VMEM((SUBSTEPS, dirs, bins, cols), f32),
            pltpu.VMEM((SUBSTEPS, dirs, bins, cols), f32),
            pltpu.VMEM((rows, bins, cols), f32),
            pltpu.VMEM((rows, bins, cols), f32),
            pltpu.VMEM((rows, bins, cols), f32),
            pltpu.VMEM((rows, 8, cols), f32),
            pltpu.VMEM((rows, 8, cols), f32),
            pltpu.SemaphoreType.DMA((SUBSTEPS, 4, parts)),
            pltpu.SemaphoreType.DMA((SUBSTEPS, 4, parts)),
            pltpu.SemaphoreType.DMA((2, 3 * parts)),
            pltpu.SemaphoreType.DMA((2,)),
            pltpu.VMEM((rows, cols), f32),
            pltpu.SMEM((2, dirs), f32),
            pltpu.VMEM((rows, cols), f32),
            pltpu.VMEM((rows, cols), jnp.int32),
            pltpu.VMEM((rows, cols), jnp.int32),
            pltpu.VMEM((rows, cols), f32),
            pltpu.SemaphoreType.DMA((4,)),
            pltpu.SemaphoreType.DMA((rows, 2)),
            pltpu.SemaphoreType.DMA((4, parts)),
            pltpu.SemaphoreType.DMA(()),
        ],
        compiler_params=pltpu.CompilerParams(
            collective_id=0, has_side_effects=True, vmem_limit_bytes=63 * 1024 * 1024
        ),
    )(
        offsets,
        weights,
        jnp.swapaxes(energy, 1, 2),
        water_depth,
        wet_mask,
        vegetation,
        canopy,
    )
    block = pl.BlockSpec((1, dirs // 2, bins, cols), lambda i: (i // 2, i % 2, 0, 0))
    whole = pl.BlockSpec((rows, cols), lambda i: (0, 0))
    moved, orbital = pl.pallas_call(
        hand_over,
        grid=(2 * rows,),
        out_shape=(
            jax.ShapeDtypeStruct(moved.shape, f32),
            jax.ShapeDtypeStruct(orbital.shape, f32),
        ),
        in_specs=[block, whole],
        out_specs=(block, whole),
        compiler_params=pltpu.CompilerParams(vmem_limit_bytes=63 * 1024 * 1024),
    )(moved, orbital)
    return jnp.swapaxes(moved, 1, 2), orbital


def body(groups, tiles, energy, *rest):
    rows, bins, dirs, cols = energy.shape
    if groups == 2 and rows == ROWS and bins % 8 == 0 and dirs % (4 * PART) == 0 and cols == 128:
        return kernel_body(groups, tiles, energy, *rest)
    return plain_body(energy, *rest)


def solution(mesh):
    placed = (
        P("geo", "freq", None, None),
        P("geo", None),
        P("geo", None),
        P("geo", None),
        P("geo", None),
        P(),
        P(),
    )
    return jax.shard_map(
        functools.partial(body, mesh.shape["freq"], mesh.shape["geo"]),
        mesh=mesh,
        in_specs=placed,
        out_specs=(P("geo", "freq", None, None), P("geo", None)),
        check_vma=False,
    )
```

```python
import functools
import math

import jax
import jax.numpy as jnp
import numpy as np
from jax import lax
from jax.experimental import pallas as pl
from jax.experimental.pallas import tpu as pltpu
from jax.sharding import PartitionSpec as P

FH = 4
SUBSTEPS = 8


gravity = 9.81
base_freq = 0.03
freq_ratio = 1.05
cell_size = 20.0
sub_step = 2.0
coupling = 0.01
coef_plus = 0.4096
coef_minus = 3.1605
coef_both = 2.589


def padded(block, sides, width):
    for axis, dim in sides:
        count = lax.axis_size(axis)
        forward = [(i, i + 1) for i in range(count - 1)]
        backward = [(target, source) for source, target in forward]
        low = lax.ppermute(
            lax.slice_in_dim(block, block.shape[dim] - width, None, axis=dim), axis, forward
        )
        high = lax.ppermute(lax.slice_in_dim(block, 0, width, axis=dim), axis, backward)
        block = jnp.concatenate([low, block, high], axis=dim)
    return block


def physics(radian_freq, water_depth, dir_count):
    square = (radian_freq * radian_freq)[None, :, None]
    column = water_depth[:, None, :]
    depth_ratio = square * column / gravity
    depth_wave = depth_ratio / jnp.sqrt(jnp.tanh(depth_ratio))
    group_speed = (
        radian_freq[None, :, None]
        * column
        / depth_wave
        * (0.5 + depth_wave / jnp.sinh(2.0 * depth_wave))
    )
    orbit_weight = (
        square
        / jnp.sinh(depth_wave) ** 2
        * (radian_freq * (freq_ratio - 1.0))[None, :, None]
        * (2.0 * math.pi / dir_count)
    )
    return (group_speed, orbit_weight)


def angles_of(dir_count):
    angles = (jnp.arange(dir_count, dtype=jnp.float32) + 0.5) * (2.0 * math.pi / dir_count)
    return (jnp.cos(angles), jnp.sin(angles))


def shifted(doubled, freq_off, dir_off, count):
    dir_count = doubled.shape[2] // 2
    starts = (
        jnp.zeros((), jnp.int32),
        freq_off + FH,
        dir_off % dir_count,
        jnp.zeros((), jnp.int32),
    )
    return lax.dynamic_slice(
        doubled, starts, (doubled.shape[0], count, dir_count, doubled.shape[3])
    )


def interaction(extended, masked, quad_offsets, quad_weights):
    count = masked.shape[1]
    doubled = jnp.concatenate([extended, extended], axis=2)
    up_bins, down_bins, up_turn, down_turn = (
        quad_offsets[0],
        quad_offsets[1],
        quad_offsets[2],
        quad_offsets[3],
    )
    weight_up, weight_down = (quad_weights[0], quad_weights[1])
    upper = weight_up * shifted(doubled, up_bins, up_turn, count) + (1.0 - weight_up) * shifted(
        doubled, up_bins + 1, up_turn, count
    )
    lower = weight_down * shifted(doubled, -down_bins, -down_turn, count) + (
        1.0 - weight_down
    ) * shifted(doubled, -down_bins - 1, -down_turn, count)
    return coupling * (
        masked * masked * (coef_plus * upper + coef_minus * lower)
        - coef_both * masked * upper * lower
    )


def redistribute(extended, transfer, quad_offsets, quad_weights):
    count = transfer.shape[1]
    doubled = jnp.concatenate([extended, extended], axis=2)
    up_bins, down_bins, up_turn, down_turn = (
        quad_offsets[0],
        quad_offsets[1],
        quad_offsets[2],
        quad_offsets[3],
    )
    weight_up, weight_down = (quad_weights[0], quad_weights[1])
    gained = weight_up * shifted(doubled, -up_bins, -up_turn, count) + (1.0 - weight_up) * shifted(
        doubled, -up_bins - 1, -up_turn, count
    )
    gained = (
        gained
        + weight_down * shifted(doubled, down_bins, down_turn, count)
        + (1.0 - weight_down) * shifted(doubled, down_bins + 1, down_turn, count)
    )
    return gained - 2.0 * transfer


def east_west(east_flux, cosines):
    zeros = jnp.zeros_like(east_flux[..., :1])
    behind = jnp.concatenate([zeros, east_flux[..., :-1]], axis=-1)
    ahead = jnp.concatenate([east_flux[..., 1:], zeros], axis=-1)
    east_going = (cosines > 0.0).astype(jnp.float32)[None, None, :, None]
    return east_going * (east_flux - behind) + (1.0 - east_going) * (ahead - east_flux)


def plain_body(energy, water_depth, wet_mask, vegetation, canopy, quad_offsets, quad_weights):
    tile_rows, freq_count, dir_count, tile_cols = energy.shape
    wet_field = wet_mask.astype(jnp.float32)
    veg_field = vegetation.astype(jnp.float32)
    wet_four = wet_field[:, None, None, :]
    masked = wet_four * energy
    first_bin = lax.axis_index("freq") * freq_count
    bin_index = (first_bin + jnp.arange(freq_count, dtype=jnp.int32)).astype(jnp.float32)
    radian_freq = 2.0 * math.pi * base_freq * jnp.power(freq_ratio, bin_index)
    group_speed, orbit_weight = physics(radian_freq, water_depth, dir_count)
    partial_value = jnp.sum(orbit_weight * jnp.sum(energy, axis=2), axis=1)
    orbital = jnp.sqrt(lax.psum(partial_value, "freq"))
    full_step = SUBSTEPS * sub_step
    damping = 1.0 + full_step * canopy * veg_field * orbital
    extended = padded(masked, (("freq", 1),), FH)
    transfer = interaction(extended, masked, quad_offsets, quad_weights)
    spread = padded(transfer, (("freq", 1),), FH)
    change = redistribute(spread, transfer, quad_offsets, quad_weights)
    increment = (masked + full_step * change) / damping[:, None, None, :] - masked
    cosines, sines = angles_of(dir_count)
    step_ratio = sub_step / cell_size
    east_speed = group_speed[:, :, None, :] * cosines[None, None, :, None]
    north_speed = group_speed[:, :, None, :] * sines[None, None, :, None]
    north_going = (sines > 0.0).astype(jnp.float32)[None, None, :, None]
    spectrum = masked
    for substep in range(SUBSTEPS):
        east_flux = east_speed * spectrum
        north_flux = north_speed * spectrum
        rimmed = padded(north_flux, (("geo", 0),), 1)
        below = rimmed[:-2]
        above = rimmed[2:]
        along = north_going * (north_flux - below) + (1.0 - north_going) * (above - north_flux)
        spectrum = wet_four * (spectrum - step_ratio * (east_west(east_flux, cosines) + along))
    return (wet_four * (spectrum + increment), orbital)


MESH = pl.DeviceIdType.MESH
ROWS = 4
REACH = 8
PART = 9


def sinh_of(x):
    square = x * x
    series = 1.0 + square / 210.0
    for term in (156.0, 110.0, 72.0, 42.0, 20.0, 6.0):
        series = 1.0 + square / term * series
    wide = jnp.exp(x)
    return jnp.where(x < 1.7, x * series, 0.5 * (wide - 1.0 / wide))


def tanh_of(x):
    low = sinh_of(jnp.minimum(x, 1.0))
    fall = jnp.exp(-2.0 * x)
    return jnp.where(x < 1.0, low / jnp.sqrt(1.0 + low * low), (1.0 - fall) / (1.0 + fall))


def kernel(
    groups,
    tiles,
    dirs,
    quad_offsets,
    quad_weights,
    coefs,
    energy,
    radian,
    depth,
    wet_mask,
    vegetation,
    canopy,
    out,
    orbital,
    ext,
    quads,
    spec,
    incr,
    inbox,
    outbox,
    fringe,
    speed,
    wet,
    drag,
    part_mine,
    part_theirs,
    send_sem,
    recv_sem,
    fringe_sems,
    part_sems,
):
    bins = energy.shape[2]
    quarter = dirs // 4
    parts = quarter // PART
    mine = lax.axis_index("freq")
    tile = lax.axis_index("geo")
    has_below = tile > 0
    has_above = tile < tiles - 1
    below_id = jnp.maximum(tile - 1, 0)
    above_id = jnp.minimum(tile + 1, tiles - 1)

    barrier = pltpu.get_barrier_semaphore()
    pl.semaphore_signal(barrier, inc=1, device_id=(1 - mine, tile), device_id_type=MESH)

    @pl.when(has_below)
    def _():
        pl.semaphore_signal(barrier, inc=1, device_id=(mine, below_id), device_id_type=MESH)

    @pl.when(has_above)
    def _():
        pl.semaphore_signal(barrier, inc=1, device_id=(mine, above_id), device_id_type=MESH)

    first = pl.multiple_of(mine * bins, 8)
    freq = radian[pl.ds(first, bins), :]
    square = freq * freq
    for row in range(ROWS):
        column = jnp.broadcast_to(depth[row : row + 1, :], (bins, 128))
        ratio = square * column / gravity
        wave = ratio / jnp.sqrt(tanh_of(ratio))
        speed[row] = (sub_step / cell_size) * (
            freq * column / wave * (0.5 + wave / sinh_of(2.0 * wave))
        )
        wet[row] = jnp.broadcast_to(wet_mask[row : row + 1, :].astype(jnp.float32), (bins, 128))

    def edge(step, q, k):
        first_dir = q * quarter + k * PART
        north = q < 2
        return pltpu.make_async_remote_copy(
            src_ref=outbox.at[step, pl.ds(first_dir, PART)],
            dst_ref=inbox.at[step, pl.ds(first_dir, PART)],
            send_sem=send_sem.at[step, q, k],
            recv_sem=recv_sem.at[step, q, k],
            device_id=(mine, above_id if north else below_id),
            device_id_type=MESH,
        )

    def sends(q):
        return has_above if q < 2 else has_below

    def receives(q):
        return has_below if q < 2 else has_above

    waits = 1 + has_below.astype(jnp.int32) + has_above.astype(jnp.int32)
    pl.semaphore_wait(barrier, waits)

    def first_edges(k, carry):
        for q in (0, 2, 1, 3):
            row = ROWS - 1 if q < 2 else 0
            for d in range(PART):
                j = q * quarter + k * PART + d
                outbox[0, j] = speed[row] * (wet[row] * energy[j, row])

            @pl.when(sends(q))
            def _():
                edge(0, q, k).start()

        return carry

    lax.fori_loop(0, parts, first_edges, 0)

    fringe_copy = pltpu.make_async_remote_copy(
        src_ref=energy.at[:, :, pl.ds(pl.multiple_of((1 - mine) * (bins - REACH), 8), REACH), :],
        dst_ref=fringe,
        send_sem=fringe_sems.at[0],
        recv_sem=fringe_sems.at[1],
        device_id=(1 - mine, tile),
        device_id_type=MESH,
    )
    fringe_copy.start()

    @pl.when(jnp.logical_not(has_below))
    def _():
        def clear(step, carry):
            inbox[step, pl.ds(0, 2 * quarter)] = jnp.zeros((2 * quarter, bins, 128), jnp.float32)
            return carry

        lax.fori_loop(0, SUBSTEPS, clear, 0)

    @pl.when(jnp.logical_not(has_above))
    def _():
        def clear(step, carry):
            inbox[step, pl.ds(2 * quarter, 2 * quarter)] = jnp.zeros(
                (2 * quarter, bins, 128), jnp.float32
            )
            return carry

        lax.fori_loop(0, SUBSTEPS, clear, 0)

    empty = pl.multiple_of(mine * (REACH + bins), 8)
    taken = pl.multiple_of((1 - mine) * (REACH + bins), 8)

    def fill(j, totals):
        sums = []
        for row in range(ROWS):
            raw = energy[j, row]
            wetted = wet[row] * raw
            spec[j, row] = wetted
            ext[j, row, REACH : REACH + bins, :] = wetted
            ext[j, row, pl.ds(empty, REACH), :] = jnp.zeros((REACH, 128), jnp.float32)
            sums.append(totals[row] + raw)
        return tuple(sums)

    totals = lax.fori_loop(
        0, dirs, fill, tuple(jnp.zeros((bins, 128), jnp.float32) for _ in range(ROWS))
    )
    for row in range(ROWS):
        column = jnp.broadcast_to(depth[row : row + 1, :], (bins, 128))
        ratio = square * column / gravity
        wave = ratio / jnp.sqrt(tanh_of(ratio))
        steep = sinh_of(wave)
        weight = (
            square / (steep * steep) * (freq * (freq_ratio - 1.0)) * (2.0 * math.pi / dirs)
        )
        part_mine[row] = jnp.broadcast_to(
            jnp.sum(weight * totals[row], axis=0, keepdims=True), (8, 128)
        )
    part_copy = pltpu.make_async_remote_copy(
        src_ref=part_mine,
        dst_ref=part_theirs,
        send_sem=part_sems.at[0],
        recv_sem=part_sems.at[1],
        device_id=(1 - mine, tile),
        device_id_type=MESH,
    )
    part_copy.start()

    lane = lax.broadcasted_iota(jnp.int32, (bins, 128), 1)

    def move(step, q, k, last):
        east = q in (0, 3)
        north = q < 2
        inside = (lane != (0 if east else 127)).astype(jnp.float32)
        order = range(ROWS) if north else range(ROWS - 1, -1, -1)
        for d in range(PART):
            j = q * quarter + k * PART + d
            across, along = coefs[0, j], coefs[1, j]
            both = across + along
            sideways = across * inside
            before = inbox[step, j]
            for row in order:
                held = spec[j, row]
                flux = speed[row] * held
                beside = pltpu.roll(flux, 1 if east else 127, 1)
                fresh = wet[row] * (held - both * flux + sideways * beside + along * before)
                before = flux
                if last:
                    out[j, row] = fresh + wet[row] * incr[j, row]
                else:
                    spec[j, row] = fresh
            if not last:
                outbox[step + 1, j] = speed[row] * fresh

    def substep(step, last=False):
        def piece(k, carry):
            for q in (0, 2, 1, 3):

                @pl.when(receives(q))
                def _():
                    edge(step, q, k).wait_recv()

                move(step, q, k, last)
                if not last:

                    @pl.when(sends(q))
                    def _():
                        edge(step + 1, q, k).start()

            return carry

        lax.fori_loop(0, parts, piece, 0)

    def plain_step(step, carry):
        substep(step)
        return carry

    lax.fori_loop(0, 3, plain_step, 0)

    part_copy.wait()
    fringe_copy.wait()

    for row in range(ROWS):
        total = jnp.sqrt(part_mine[row] + part_theirs[row])
        orbital[row : row + 1, :] = total[0:1, :]
        leaves = vegetation[row : row + 1, :].astype(jnp.float32) * canopy[row : row + 1, :]
        damping = 1.0 + (SUBSTEPS * sub_step) * leaves * total[0:1, :]
        drag[row] = jnp.broadcast_to(1.0 / damping, (bins, 128))

    def take(j, carry):
        for row in range(ROWS):
            ext[j, row, pl.ds(taken, REACH), :] = wet[row, 0:REACH, :] * fringe[j, row]
        return carry

    lax.fori_loop(0, dirs, take, 0)

    up_bins, up_turn, down_turn = quad_offsets[0], quad_offsets[2], quad_offsets[3]
    weight_up, weight_down = quad_weights[0], quad_weights[1]
    rest_up, rest_down = 1.0 - weight_up, 1.0 - weight_down
    half = REACH // 2
    span = bins + REACH

    def turned(j, turn):
        j = j + turn
        j = jnp.where(j >= dirs, j - dirs, j)
        return jnp.where(j < 0, j + dirs, j)

    def couple(j, carry):
        high, low = turned(j, up_turn), turned(j, -down_turn)
        for row in range(ROWS):
            here = ext[j, row, half : half + span, :]
            upper = (
                weight_up * ext[high, row, pl.ds(half + up_bins, span), :]
                + rest_up * ext[high, row, pl.ds(half + up_bins + 1, span), :]
            )
            lower = (
                weight_down * ext[low, row, half - 3 : half - 3 + span, :]
                + rest_down * ext[low, row, half - 4 : half - 4 + span, :]
            )
            quads[j, row] = (coupling * here) * (
                here * (coef_plus * upper + coef_minus * lower) - coef_both * (upper * lower)
            )
        return carry

    def spread(j, carry):
        back, ahead = turned(j, -up_turn), turned(j, down_turn)
        for row in range(ROWS):
            change = (
                weight_up * quads[back, row, pl.ds(half - up_bins, bins), :]
                + rest_up * quads[back, row, pl.ds(half - up_bins - 1, bins), :]
                + weight_down * quads[ahead, row, half + 3 : half + 3 + bins, :]
                + rest_down * quads[ahead, row, half + 4 : half + 4 + bins, :]
                - 2.0 * quads[j, row, half : half + bins, :]
            )
            wetted = ext[j, row, REACH : REACH + bins, :]
            incr[j, row] = (wetted + (SUBSTEPS * sub_step) * change) * drag[row] - wetted
        return carry

    def couple_step(step, carry):
        substep(step)
        lax.fori_loop((step - 3) * (dirs // 2), (step - 2) * (dirs // 2), couple, 0)
        return carry

    def spread_step(step, carry):
        substep(step)
        lax.fori_loop((step - 5) * (dirs // 2), (step - 4) * (dirs // 2), spread, 0)
        return carry

    lax.fori_loop(3, 5, couple_step, 0)
    lax.fori_loop(5, 7, spread_step, 0)
    substep(SUBSTEPS - 1, last=True)

    def drain(step, carry):
        def piece(k, inner):
            for q in range(4):

                @pl.when(sends(q))
                def _():
                    edge(step, q, k).wait_send()

            return inner

        return lax.fori_loop(0, parts, piece, carry)

    lax.fori_loop(0, SUBSTEPS, drain, 0)


def kernel_body(groups, tiles, energy, water_depth, wet_mask, vegetation, canopy, offsets, weights):
    rows, bins, dirs, cols = energy.shape
    angles = (np.arange(dirs, dtype=np.float32) + np.float32(0.5)) * np.float32(
        2.0 * math.pi / dirs
    )
    coefs = np.abs(np.stack([np.cos(angles), np.sin(angles)])).astype(np.float32)
    radian = 2.0 * math.pi * base_freq * freq_ratio ** np.arange(groups * bins)
    radian = np.broadcast_to(radian.astype(np.float32)[:, None], (groups * bins, cols))
    vmem = pl.BlockSpec(memory_space=pltpu.VMEM)
    smem = pl.BlockSpec(memory_space=pltpu.SMEM)
    f32 = jnp.float32
    parts = dirs // 4 // PART
    moved, orbital = pl.pallas_call(
        functools.partial(kernel, groups, tiles, dirs),
        out_shape=(
            jax.ShapeDtypeStruct((dirs, rows, bins, cols), f32),
            jax.ShapeDtypeStruct((rows, cols), f32),
        ),
        in_specs=[smem] * 3 + [vmem] * 6,
        out_specs=(vmem, vmem),
        scratch_shapes=[
            pltpu.VMEM((dirs, rows, bins + 2 * REACH, cols), f32),
            pltpu.VMEM((dirs, rows, bins + REACH, cols), f32),
            pltpu.VMEM((dirs, rows, bins, cols), f32),
            pltpu.VMEM((dirs, rows, bins, cols), f32),
            pltpu.VMEM((SUBSTEPS, dirs, bins, cols), f32),
            pltpu.VMEM((SUBSTEPS, dirs, bins, cols), f32),
            pltpu.VMEM((dirs, rows, REACH, cols), f32),
            pltpu.VMEM((rows, bins, cols), f32),
            pltpu.VMEM((rows, bins, cols), f32),
            pltpu.VMEM((rows, bins, cols), f32),
            pltpu.VMEM((rows, 8, cols), f32),
            pltpu.VMEM((rows, 8, cols), f32),
            pltpu.SemaphoreType.DMA((SUBSTEPS, 4, parts)),
            pltpu.SemaphoreType.DMA((SUBSTEPS, 4, parts)),
            pltpu.SemaphoreType.DMA((2,)),
            pltpu.SemaphoreType.DMA((2,)),
        ],
        compiler_params=pltpu.CompilerParams(
            collective_id=0, has_side_effects=True, vmem_limit_bytes=48 * 1024 * 1024
        ),
    )(
        offsets,
        weights,
        jnp.asarray(coefs),
        jnp.transpose(energy, (2, 0, 1, 3)),
        jnp.asarray(radian),
        water_depth,
        wet_mask,
        vegetation,
        canopy,
    )
    return jnp.transpose(moved, (1, 2, 0, 3)), orbital


def body(groups, tiles, energy, *rest):
    rows, bins, dirs, cols = energy.shape
    if groups == 2 and rows == ROWS and bins % 8 == 0 and dirs % (4 * PART) == 0 and cols == 128:
        return kernel_body(groups, tiles, energy, *rest)
    return plain_body(energy, *rest)


def solution(mesh):
    placed = (
        P("geo", "freq", None, None),
        P("geo", None),
        P("geo", None),
        P("geo", None),
        P("geo", None),
        P(),
        P(),
    )
    return jax.shard_map(
        functools.partial(body, mesh.shape["freq"], mesh.shape["geo"]),
        mesh=mesh,
        in_specs=placed,
        out_specs=(P("geo", "freq", None, None), P("geo", None)),
        check_vma=False,
    )
```
